256 devices in a mesh: seq: 16 (over z, core), head: 4 (over x), dp: 4 (over y).
Axes of the slice: x: 4, y: 4, z: 8, core: 2. Of those that a mesh axis runs over, the one named last changes fastest.
Arguments:
- queries: bfloat16 [4, 768, 32768], P('dp', 'head', 'seq'), may hold values from -170 to 170
- keys: bfloat16 [4, 768, 32768], P('dp', 'head', 'seq'), may hold values from -4 to 4
- values: bfloat16 [4, 768, 32768], P('dp', 'head', 'seq'), may hold values from -4 to 4
- cotangent: bfloat16 [4, 768, 32768], P('dp', 'head', 'seq'), may hold values from -5 to 5
- w_out: bfloat16 [768, 768], P('head'), may hold values from -0.21875 to 0.21875
- lengths: int32 [4], P('dp'), may hold values from 8192 to 32768, as said below
- offsets: int32 [12], P('head'), may hold values from 0 to 15
Outputs:
- mixed: bfloat16 [4, 768, 32768], P('dp', 'head', 'seq')
- query_grad: bfloat16 [4, 768, 32768], P('dp', 'head', 'seq')
- key_grad: bfloat16 [4, 768, 32768], P('dp', 'head', 'seq')
- value_grad: bfloat16 [4, 768, 32768], P('dp', 'head', 'seq')
- weight_grad: float32 [768, 768], P('head')
The draws below stay inside these ranges and needn't reach their ends.
Inputs may be any that keep to these rules, and one draw needn't show every extreme that they name: `lengths`: one slide in every draw has all 32768 positions.
All inputs are finite; a program needn't handle non-finite values.
Results may differ from the reference program's by a relative error of at most 0.013.
Values may be sent and summed in bfloat16 or wider, within the bound.
No kernel may reach another device: no remote copies, remote signals or barrier semaphores. Data moves between devices by JAX's collectives and lax.ppermute only.
A program may use at most 192 MiB of HBM per device.

```python
import math
import jax
import jax.numpy as jnp
from jax import lax

D = 768
HEADS = 12
SEL = 2048
TOKENS = 32768
SLIDES = 4
N_HEAD = 4


def shared_keys(key):
    return jnp.clip(jax.random.normal(key, (SLIDES, D, TOKENS), jnp.float32), -4.0, 4.0)


def draw_keys(key, part):
    base_keys = shared_keys(key)
    return base_keys.astype(jnp.bfloat16)


def draw_queries(key, part):
    key = jax.random.fold_in(key, 7)
    first_key = jax.random.fold_in(key, 0)
    noise = jnp.clip(jax.random.normal(first_key, (SLIDES, D, TOKENS), jnp.float32), -4.0, 4.0)
    return (2.0 * noise).astype(jnp.bfloat16)


def draw_lengths(key, part):
    key = jax.random.fold_in(key, 11)
    first_key, second_key = jax.random.split(key)
    short_lengths = jax.random.randint(first_key, (SLIDES,), TOKENS // 4, TOKENS + 1)
    longest = jax.random.randint(second_key, (), 0, SLIDES)
    return jnp.where(jnp.arange(SLIDES) == longest, TOKENS, short_lengths).astype(jnp.int32)


def plant(values, own_key, low, largest):
    spot = [jax.random.randint(jax.random.fold_in(own_key, axis), (), 0, length) for axis, length in enumerate(values.shape)]
    main_axis = values.shape.index(max(values.shape))
    neighbour = spot[:main_axis] + [(spot[main_axis] + 1) % values.shape[main_axis]] + spot[main_axis + 1:]
    return values.at[tuple(spot)].set(low).at[tuple(neighbour)].set(largest)


def shard_levels(stream_key, shape, cuts, low, high):
    gain = 1.0
    for position, shards_of in cuts:
        heights = jax.random.uniform(jax.random.fold_in(jax.random.fold_in(stream_key, 6), position), (shards_of,), jnp.float32, low / len(cuts), high / len(cuts))
        gain = gain * jnp.repeat(jnp.exp(heights), shape[position] // shards_of).reshape((-1,) + (1,) * (len(shape) - 1 - position))
    return gain


def centred(stream_key, shape, spread, bound, pieces=(), kind=jnp.bfloat16):
    gain = shard_levels(stream_key, shape, pieces, -0.22, 0.18) if pieces else 1.0
    array = jax.random.normal(stream_key, shape, jnp.float32) * spread * gain
    return jnp.minimum(jnp.maximum(array, -bound), bound).astype(kind)


def setup_inputs(seed: int = 0) -> dict:
    key_list = jax.random.split(jax.random.key(seed), 8)
    queries = draw_queries(jax.random.fold_in(key_list[7], 71), 0)
    keys = draw_keys(jax.random.fold_in(key_list[7], 71), 0)
    values = centred(key_list[2], (SLIDES, D, TOKENS), 1.0, 4.0, ((0, 4), (1, 4), (2, 16)))
    cotangent = centred(key_list[3], (SLIDES, D, TOKENS), 1.0, 5.0, ((0, 4), (1, 4), (2, 16)))
    w_out = centred(key_list[4], (D, D), D ** -0.5, 0.21875, ((0, 4),))
    lengths = draw_lengths(jax.random.fold_in(key_list[7], 71), 0)
    offsets = plant(jax.random.randint(key_list[6], (HEADS,), 0, TOKENS // SEL), jax.random.fold_in(key_list[6], 1), 0, (TOKENS // SEL) - 1).astype(jnp.int32)
    return {"queries": queries, "keys": keys, "values": values, "cotangent": cotangent, "w_out": w_out, "lengths": lengths, "offsets": offsets}


NEGATIVE = -1e+30

def attend(q_rows, k_rows, v_rows, keep_keys):
    factor = q_rows.shape[-1] ** (-0.5)
    scores = jnp.einsum('hqe,hke->hqk', q_rows.astype(jnp.float32), k_rows.astype(jnp.float32)) * factor
    scores = jnp.where(keep_keys[:, None, :], scores, NEGATIVE)
    row_top = lax.optimization_barrier(jnp.max(scores, axis=-1, keepdims=True))
    expo_terms = jnp.exp(scores - row_top)
    row_total = lax.optimization_barrier(jnp.sum(expo_terms, axis=-1, keepdims=True))
    row_probs = expo_terms / row_total
    weights = lax.optimization_barrier(row_probs.astype(jnp.bfloat16))
    result = jnp.einsum('hqk,hke->hqe', weights.astype(jnp.float32), v_rows.astype(jnp.float32))
    return (result, (row_top + jnp.log(row_total))[..., 0], row_probs, weights)

def attend_back(q_rows, k_rows, v_rows, keep_keys, grad_out, grad_lse):
    factor = q_rows.shape[-1] ** (-0.5)
    unused_out, unused_lse, row_probs, weights = attend(q_rows, k_rows, v_rows, keep_keys)
    grad_bf = lax.optimization_barrier(grad_out.astype(jnp.bfloat16))
    grad_v = jnp.einsum('hqk,hqe->hke', weights.astype(jnp.float32), grad_bf.astype(jnp.float32))
    grad_prob = jnp.einsum('hqe,hke->hqk', grad_bf.astype(jnp.float32), v_rows.astype(jnp.float32))
    delta_row = lax.optimization_barrier(jnp.sum(row_probs * grad_prob, axis=-1))
    grad_score = (row_probs * (grad_prob - delta_row[..., None] + grad_lse[..., None]) * factor).astype(jnp.bfloat16)
    grad_score = lax.optimization_barrier(grad_score)
    grad_q = jnp.einsum('hqk,hke->hqe', grad_score.astype(jnp.float32), k_rows.astype(jnp.float32))
    grad_k = jnp.einsum('hqk,hqe->hke', grad_score.astype(jnp.float32), q_rows.astype(jnp.float32))
    return (grad_q, grad_k, grad_v, delta_row)

def select_rows(source, offsets, sel_rate):
    heads_here, count = (source.shape[0], source.shape[1])
    grid = source.reshape((heads_here, count // sel_rate, sel_rate) + source.shape[2:])
    picker = offsets.astype(jnp.int32).reshape((heads_here, 1, 1) + (1,) * (source.ndim - 2))
    return jnp.take_along_axis(grid, picker, axis=2)[:, :, 0]

def place_rows(source, offsets, sel_rate):
    heads_here, count = (source.shape[0], source.shape[1])
    hits = (jnp.arange(sel_rate, dtype=jnp.int32)[None, :] == offsets[:, None]).astype(source.dtype)
    hits = hits.reshape((heads_here, 1, sel_rate) + (1,) * (source.ndim - 2))
    return (source[:, :, None] * hits).reshape((heads_here, count * sel_rate) + source.shape[2:])

def segments(source):
    heads_here, count = (source.shape[0], source.shape[1])
    return jnp.moveaxis(source.reshape((heads_here, count // SEL, SEL) + source.shape[2:]), 1, 0)

def unsegment(stacked):
    moved = jnp.moveaxis(stacked, 0, 1)
    return moved.reshape((moved.shape[0], moved.shape[1] * moved.shape[2]) + moved.shape[3:])

def local_forward(q_heads, k_heads, v_heads, keep_rows):

    def one_segment(items):
        result, lse_part, unused_probs, unused_weights = attend(*items)
        return (result, lse_part)
    results, lse_parts = lax.map(one_segment, tuple((segments(x) for x in (q_heads, k_heads, v_heads, keep_rows))))
    return (unsegment(results), unsegment(lse_parts))

def local_backward(q_heads, k_heads, v_heads, keep_rows, dout, dlse):

    def one_segment(items):
        grad_q, grad_k, grad_v, unused_delta = attend_back(*items)
        return (grad_q, grad_k, grad_v)
    stacked = lax.map(one_segment, tuple((segments(x) for x in (q_heads, k_heads, v_heads, keep_rows, dout, dlse))))
    return tuple((unsegment(x) for x in stacked))

def one_slide(query_rows, key_rows, value_rows, dy_rows, length, offsets, w_out):
    count = query_rows.shape[0]
    heads_here = offsets.shape[0]
    head_dim = query_rows.shape[1] // heads_here
    sel_rate = count // SEL

    def split_heads(source):
        return source.reshape(count, heads_here, head_dim).transpose(1, 0, 2)

    def join_heads(source):
        return source.transpose(1, 0, 2).reshape(count, heads_here * head_dim)
    q_heads, k_heads, v_heads = (split_heads(query_rows), split_heads(key_rows), split_heads(value_rows))
    keep_row = jnp.arange(count, dtype=jnp.int32) < length
    keep_rows = jnp.broadcast_to(keep_row[None, :], (heads_here, count))
    out_near, lse_near = local_forward(q_heads, k_heads, v_heads, keep_rows)
    q_pick = select_rows(q_heads, offsets, sel_rate)
    k_pick = select_rows(k_heads, offsets, sel_rate)
    v_pick = select_rows(v_heads, offsets, sel_rate)
    keep_pick = select_rows(keep_rows, offsets, sel_rate)
    out_pick, lse_pick, unused_probs, unused_weights = attend(q_pick, k_pick, v_pick, keep_pick)
    chosen = place_rows(jnp.ones_like(lse_pick), offsets, sel_rate) > 0
    out_far = place_rows(out_pick, offsets, sel_rate)
    lse_far = jnp.where(chosen, place_rows(lse_pick, offsets, sel_rate), NEGATIVE)
    share_near = jax.nn.sigmoid(lse_near - lse_far)
    share_far = jax.nn.sigmoid(lse_far - lse_near)
    live_rows = keep_rows.astype(jnp.float32)[..., None]
    head_outs = (share_near[..., None] * out_near + share_far[..., None] * out_far) * live_rows
    attn_rows = join_heads(head_outs).astype(jnp.bfloat16)
    group = w_out.shape[0] // N_HEAD
    summed = jnp.zeros((count, w_out.shape[1]), jnp.float32)
    for number in range(N_HEAD):
        piece = jnp.dot(attn_rows[:, number * group:(number + 1) * group], w_out[number * group:(number + 1) * group], preferred_element_type=jnp.float32)
        summed = summed + piece.astype(jnp.bfloat16).astype(jnp.float32)
    mixed = summed.astype(jnp.bfloat16)
    d_attn = jnp.dot(dy_rows, w_out.T, preferred_element_type=jnp.float32).astype(jnp.bfloat16)
    weight_part = jnp.dot(attn_rows.T, dy_rows, preferred_element_type=jnp.float32)
    grad_rows = split_heads(d_attn).astype(jnp.float32) * live_rows
    dout_near = share_near[..., None] * grad_rows
    dout_far = share_far[..., None] * grad_rows
    dlse_near = share_near * share_far * lax.optimization_barrier(jnp.sum(grad_rows * (out_near - out_far), axis=-1))
    dout_pick = select_rows(dout_far, offsets, sel_rate)
    dlse_pick = -select_rows(dlse_near, offsets, sel_rate)
    dq_near, dk_near, dv_near = local_backward(q_heads, k_heads, v_heads, keep_rows, dout_near, dlse_near)
    dq_pick, dk_pick, dv_pick, unused_delta = attend_back(q_pick, k_pick, v_pick, keep_pick, dout_pick, dlse_pick)

    def merge_grads(near_part, far_part):
        return join_heads(near_part + place_rows(far_part, offsets, sel_rate)).astype(jnp.bfloat16)
    return (mixed, merge_grads(dq_near, dq_pick), merge_grads(dk_near, dk_pick), merge_grads(dv_near, dv_pick), weight_part)

def reference(queries, keys, values, cotangent, w_out, lengths, offsets):
    outputs = [one_slide(queries[number].T, keys[number].T, values[number].T, cotangent[number].T, lengths[number], offsets, w_out) for number in range(queries.shape[0])]
    mixed = jnp.stack([item[0].T for item in outputs])
    query_grad = jnp.stack([item[1].T for item in outputs])
    key_grad = jnp.stack([item[2].T for item in outputs])
    value_grad = jnp.stack([item[3].T for item in outputs])
    weight_sum = outputs[0][4]
    for item in outputs[1:]:
        weight_sum = weight_sum + item[4]
    weight_grad = weight_sum * jnp.float32(1.0 / math.sqrt(TOKENS * SLIDES))
    return (mixed, query_grad, key_grad, value_grad, weight_grad)
```

```python
import math

import jax
import jax.numpy as jnp
from jax import lax
from jax.experimental import pallas as pl
from jax.experimental.pallas import tpu as pltpu
from jax.sharding import PartitionSpec as P

SEL = 2048
HD = 64
NEGATIVE = -1e30
BF = jnp.bfloat16
F32 = jnp.float32
QB = 512
VMEM_BYTES = 60 * 2**20


def dot(a, b, ca, cb):
    return lax.dot_general(a, b, (((ca,), (cb,)), ((), ())), preferred_element_type=F32)


def split2(x):
    hi = x.astype(BF)
    return hi, (x - hi.astype(F32)).astype(BF)


def split3(x):
    hi = x.astype(BF)
    rest = x - hi.astype(F32)
    mid = rest.astype(BF)
    return hi, mid, (rest - mid.astype(F32)).astype(BF)


def call(kern, name, grid, in_specs, out_specs, out_shape, scratch=(), flops=0, nbytes=0):
    return pl.pallas_call(
        kern,
        name=name,
        grid=grid,
        in_specs=in_specs,
        out_specs=out_specs,
        out_shape=out_shape,
        scratch_shapes=list(scratch),
        compiler_params=pltpu.CompilerParams(vmem_limit_bytes=VMEM_BYTES),
        cost_estimate=pl.CostEstimate(flops=flops, bytes_accessed=nbytes, transcendentals=0),
    )


SMEM = pl.BlockSpec(memory_space=pltpu.SMEM)
WHOLE = pl.BlockSpec(memory_space=pltpu.VMEM)


def sel_matrix(off, rate, rows, cols):
    pos = lax.broadcasted_iota(jnp.int32, (rows, cols), 0)
    num = lax.broadcasted_iota(jnp.int32, (rows, cols), 1)
    return jnp.where(pos == num * rate + off, 1.0, 0.0).astype(BF)


def place_matrix(off, rate, start, rows, cols):
    num = lax.broadcasted_iota(jnp.int32, (rows, cols), 0)
    pos = lax.broadcasted_iota(jnp.int32, (rows, cols), 1) + start
    return jnp.where(pos == num * rate + off, 1.0, 0.0).astype(BF)


def pick_kernel(rate, offs, q, k, v, qp, kvp):
    heads = q.shape[0] // HD
    picks = qp.shape[1]
    for h in range(heads):
        rows = slice(h * HD, (h + 1) * HD)
        sel = sel_matrix(offs[h], rate, q.shape[1], picks)
        got = dot(jnp.concatenate([q[rows, :], k[rows, :], v[rows, :]], axis=0), sel, 1, 0)
        got = got.astype(BF)
        qp[rows, :] = got[:HD]
        kvp[rows, :] = got[HD : 2 * HD]
        kvp[heads * HD + h * HD : heads * HD + (h + 1) * HD, :] = got[2 * HD :]


def stack_rows(count, parts):
    row = lax.broadcasted_iota(jnp.int32, (count, parts[0].shape[1]), 0)
    out = jnp.zeros(row.shape, F32)
    for i, part in enumerate(parts):
        out = jnp.where(row == i, part.astype(F32), out)
    return out.astype(BF)


def fwd_kernel(info, q, k, v, e_out, out, stats, kt, s_buf):
    tok = k.shape[1]
    qb = q.shape[1]

    @pl.when(pl.program_id(1) == 0)
    def _():
        pos = lax.broadcasted_iota(jnp.int32, (HD, tok), 1) + info[1]
        row = lax.broadcasted_iota(jnp.int32, (HD, tok), 0)
        bias = jnp.where((row == 0) & (pos >= info[0]), NEGATIVE, 0.0).astype(BF)
        kt[...] = jnp.concatenate([k[...], bias], axis=0).T

    one = jnp.where(lax.broadcasted_iota(jnp.int32, (HD, qb), 0) == 0, 1.0, 0.0).astype(BF)
    qa = jnp.concatenate([q[...] * jnp.asarray(0.125, BF), one], axis=0)
    row16 = lax.broadcasted_iota(jnp.int32, (16, tok), 0)
    va = jnp.concatenate([v[...], jnp.where(row16 == 0, 1.0, 0.0).astype(BF)], axis=0)
    ck = 256
    half = 256
    for c0 in range(0, qb, half):
        cols = slice(c0, c0 + half)
        top = None
        for i in range(0, tok, ck):
            s = dot(kt[i : i + ck, :], qa[:, cols], 1, 0)
            s_buf[i : i + ck, cols] = s
            part = jnp.max(s.reshape(ck // 8, 8, half), axis=0)
            top = part if top is None else jnp.maximum(top, part)
        m = jnp.max(top, axis=0, keepdims=True)
        acc = None
        for i in range(0, tok, ck):
            e = jnp.exp(s_buf[i : i + ck, cols] - m).astype(BF)
            e_out[0, i : i + ck, cols] = e
            part = dot(va[:, i : i + ck], e, 1, 0)
            acc = part if acc is None else acc + part
        t = acc[HD : HD + 1]
        rt = 1.0 / t
        out[:, cols] = acc[:HD] * rt
        stats[0, :, cols] = jnp.concatenate(
            [m + jnp.log(t), rt, jnp.zeros((6, half), F32)], axis=0
        )


def mida_kernel(rate, info, offs, qp, kvf, out_a, stats, w, terms, attn, shares, out_b, pf):
    heads = stats.shape[0]
    tok = out_a.shape[1]
    picks = qp.shape[1]
    ranks = kvf.shape[0]
    width = heads * HD
    length, start = info[0], info[1]
    pos = lax.broadcasted_iota(jnp.int32, (1, tok), 1) + start
    keep = jnp.where(pos < length, 1.0, 0.0)
    key_pos = lax.broadcasted_iota(jnp.int32, (ranks * picks, 1), 0) * rate
    for h in range(heads):
        rows = slice(h * HD, (h + 1) * HD)
        off = offs[h]
        kf = jnp.concatenate([kvf[r, rows, :] for r in range(ranks)], axis=1)
        vf = jnp.concatenate(
            [kvf[r, width + h * HD : width + (h + 1) * HD, :] for r in range(ranks)], axis=1
        )
        s = dot(kf, qp[rows, :] * jnp.asarray(0.125, BF), 0, 0)
        s = jnp.where(key_pos + off < length, s, NEGATIVE)
        m = jnp.max(s, axis=0, keepdims=True)
        e = jnp.exp(s - m)
        t = jnp.sum(e, axis=0, keepdims=True)
        p = (e * (1.0 / t)).astype(BF)
        pf[h] = p
        ob = dot(vf, p, 1, 0)
        out_b[rows, :] = ob
        lse_b = m + jnp.log(t)
        place = place_matrix(off, rate, 0, picks, tok)
        l_hi, l_mid, l_lo = split3(lse_b)
        o_hi, o_lo = split2(ob)
        stack = jnp.concatenate([o_hi, o_lo, stack_rows(16, [l_hi, l_mid, l_lo])], axis=0)
        spread = dot(stack, place, 1, 0)
        of = spread[:HD] + spread[HD : 2 * HD]
        lf = spread[128:129] + spread[129:130] + spread[130:131]
        here = lax.broadcasted_iota(jnp.int32, (1, tok), 1)
        chosen = (here % rate) == off
        lf = jnp.where(chosen, lf, NEGATIVE)
        gap = stats[h, 0:1, :] - lf
        sa = 1.0 / (1.0 + jnp.exp(-gap))
        sb = 1.0 / (1.0 + jnp.exp(gap))
        shares[h] = jnp.concatenate([sa, sb, jnp.zeros((6, tok), F32)], axis=0)
        attn[rows, :] = ((sa * out_a[rows, :] + sb * of) * keep).astype(BF)
    terms[...] = dot(w[...], attn[...], 0, 0).astype(BF)


def midb_kernel(
    rate, info, offs, cot, w, attn, shares, out_a, stats, out_b, pf, qp, kvf,
    dob, dkv, dqf, wpart,
):
    heads = stats.shape[0]
    tok = out_a.shape[1]
    picks = qp.shape[1]
    ranks = kvf.shape[0]
    width = heads * HD
    length, start = info[0], info[1]
    pos = lax.broadcasted_iota(jnp.int32, (1, tok), 1) + start
    keep = jnp.where(pos < length, 1.0, 0.0).astype(BF)
    wpart[...] = dot(attn[...], cot[...], 1, 1)
    for h in range(heads):
        rows = slice(h * HD, (h + 1) * HD)
        off = offs[h]
        g_bf = dot(w[rows, :], cot[...], 1, 0).astype(BF) * keep
        g = g_bf.astype(F32)
        place = place_matrix(off, rate, 0, picks, tok)
        sel = sel_matrix(off, rate, tok, picks)
        ob = out_b[rows, :]
        o_hi, o_lo = split2(ob)
        spread = dot(jnp.concatenate([o_hi, o_lo], axis=0), place, 1, 0)
        of = spread[:HD] + spread[HD:]
        sa, sb = shares[h, 0:1, :], shares[h, 1:2, :]
        oa = out_a[rows, :]
        dlse = sa * sb * jnp.sum(g * (oa - of), axis=0, keepdims=True)
        rt = stats[h, 1:2, :]
        dout = sa * g
        delta = jnp.sum(dout.astype(BF).astype(F32) * oa, axis=0, keepdims=True)
        c_hi, c_lo = split2((dlse - delta) * rt)
        dob[h] = jnp.concatenate(
            [(dout * rt).astype(BF), stack_rows(HD, [c_hi, c_lo])], axis=0
        )
        s_hi, s_lo = split2(sb)
        l_hi, l_lo = split2(dlse)
        picked = dot(
            jnp.concatenate([g_bf, stack_rows(16, [s_hi, s_lo, l_hi, l_lo])], axis=0), sel, 1, 0
        )
        sb_p = picked[64:65] + picked[65:66]
        dlse_p = -(picked[66:67] + picked[67:68])
        do_b = (sb_p * picked[:HD]).astype(BF)
        delta_b = jnp.sum(do_b.astype(F32) * ob, axis=0, keepdims=True)
        kf = jnp.concatenate([kvf[r, rows, :] for r in range(ranks)], axis=1)
        vf = jnp.concatenate(
            [kvf[r, width + h * HD : width + (h + 1) * HD, :] for r in range(ranks)], axis=1
        )
        dp = dot(vf, do_b, 0, 0) + (dlse_p - delta_b)
        p = pf[h]
        ds = (p.astype(F32) * dp * 0.125).astype(BF)
        dqf[rows, :] = dot(kf, ds, 1, 0)
        dk = dot(qp[rows, :], ds, 1, 1).astype(BF)
        dv = dot(do_b, p, 1, 1).astype(BF)
        for r in range(ranks):
            cols = slice(r * picks, (r + 1) * picks)
            dkv[r, rows, :] = dk[:, cols]
            dkv[r, width + h * HD : width + (h + 1) * HD, :] = dv[:, cols]


def bwd_kernel(rate, offs, e, dob, q, k, v, dqf, dq, dk, dv, vt):
    tok = k.shape[1]
    qb = q.shape[1]
    step = pl.program_id(1)

    @pl.when(step == 0)
    def _():
        row = lax.broadcasted_iota(jnp.int32, (HD, tok), 0)
        ones = jnp.where(row < 2, 1.0, 0.0).astype(BF)
        vt[...] = jnp.concatenate([v[...], ones], axis=0).T
        dk[...] = jnp.zeros_like(dk)
        dv[...] = jnp.zeros_like(dv)

    ck = 256
    do = dob[0, :HD, :]
    acc = None
    for i in range(0, tok, ck):
        dp = dot(vt[i : i + ck, :], dob[0], 1, 0)
        ei = e[0, i : i + ck, :]
        ds = (ei.astype(F32) * dp).astype(BF)
        part = dot(k[:, i : i + ck], ds, 1, 0)
        acc = part if acc is None else acc + part
        dk[:, i : i + ck] += dot(q[...], ds, 1, 1)
        dv[:, i : i + ck] += dot(do, ei, 1, 1)
    place = place_matrix(offs[pl.program_id(0)], rate, step * qb, dqf.shape[1], qb)
    d_hi, d_lo = split2(dqf[...])
    spread = dot(jnp.concatenate([d_hi, d_lo], axis=0), place, 1, 0)
    dq[...] = (acc * 0.125 + spread[:HD] + spread[HD:]).astype(BF)


def merge_kernel(rate, offs, dk, dv, far, kg, vg):
    heads = dk.shape[0] // HD
    width = heads * HD
    tok = dk.shape[1]
    picks = far.shape[2]
    total = far[0].astype(F32)
    for r in range(1, far.shape[0]):
        total = total + far[r].astype(F32)
    for h in range(heads):
        rows = slice(h * HD, (h + 1) * HD)
        place = place_matrix(offs[h], rate, 0, picks, tok)
        both = jnp.concatenate(
            [total[rows], total[width + h * HD : width + (h + 1) * HD]], axis=0
        )
        hi, lo = split2(both)
        spread = dot(jnp.concatenate([hi, lo], axis=0), place, 1, 0)
        near_k = dk[rows, :] * 0.125
        kg[rows, :] = (near_k + spread[:HD] + spread[2 * HD : 3 * HD]).astype(BF)
        vg[rows, :] = (dv[rows, :] + spread[HD : 2 * HD] + spread[3 * HD :]).astype(BF)


SDS = jax.ShapeDtypeStruct


def pick(rate, offs, q, k, v, picks):
    rows, tok = q.shape
    return call(
        lambda *r: pick_kernel(rate, *r), "pick", (), [SMEM, WHOLE, WHOLE, WHOLE], [WHOLE, WHOLE],
        [SDS((rows, picks), BF), SDS((2 * rows, picks), BF)],
        flops=6 * rows * tok * picks, nbytes=6 * rows * tok,
    )(offs, q, k, v)


def forward(info, q, k, v):
    rows, tok = q.shape
    heads = rows // HD
    qb = min(QB, tok)
    by_q = pl.BlockSpec((HD, qb), lambda h, j: (h, j))
    whole = pl.BlockSpec((HD, tok), lambda h, j: (h, 0))
    return call(
        fwd_kernel, "fwd", (heads, tok // qb), [SMEM, by_q, whole, whole],
        [
            pl.BlockSpec((1, tok, qb), lambda h, j: (h, 0, j)),
            by_q,
            pl.BlockSpec((1, 8, qb), lambda h, j: (h, 0, j)),
        ],
        [SDS((heads, tok, tok), BF), SDS((rows, tok), F32), SDS((heads, 8, tok), F32)],
        scratch=[pltpu.VMEM((tok, 2 * HD), BF), pltpu.VMEM((tok, qb), F32)],
        flops=4 * rows * tok * tok, nbytes=2 * heads * tok * tok,
    )(info, q, k, v)


def mid_a(rate, info, offs, qp, kvf, out_a, stats, w):
    rows, tok = out_a.shape
    heads = rows // HD
    picks = qp.shape[1]
    return call(
        lambda *r: mida_kernel(rate, *r), "mida", (), [SMEM, SMEM] + [WHOLE] * 5, [WHOLE] * 5,
        [
            SDS((w.shape[1], tok), BF), SDS((rows, tok), BF), SDS((heads, 8, tok), F32),
            SDS((rows, picks), F32), SDS((heads, kvf.shape[0] * picks, picks), BF),
        ],
        flops=2 * rows * tok * w.shape[1], nbytes=2 * tok * w.shape[1],
    )(info, offs, qp, kvf, out_a, stats, w)


def mid_b(rate, info, offs, cot, w, attn, shares, out_a, stats, out_b, pf, qp, kvf):
    rows, tok = out_a.shape
    heads = rows // HD
    picks = qp.shape[1]
    return call(
        lambda *r: midb_kernel(rate, *r), "midb", (), [SMEM, SMEM] + [WHOLE] * 10, [WHOLE] * 4,
        [
            SDS((heads, 2 * HD, tok), BF), SDS(kvf.shape, BF), SDS((rows, picks), F32),
            SDS(w.shape, F32),
        ],
        flops=4 * rows * tok * w.shape[1], nbytes=2 * tok * w.shape[1],
    )(info, offs, cot, w, attn, shares, out_a, stats, out_b, pf, qp, kvf)


def backward(rate, offs, e, dob, q, k, v, dqf):
    rows, tok = q.shape
    heads = rows // HD
    qb = min(QB, tok)
    by_q = pl.BlockSpec((HD, qb), lambda h, j: (h, j))
    whole = pl.BlockSpec((HD, tok), lambda h, j: (h, 0))
    return call(
        lambda *r: bwd_kernel(rate, *r), "bwd", (heads, tok // qb),
        [
            SMEM, pl.BlockSpec((1, tok, qb), lambda h, j: (h, 0, j)),
            pl.BlockSpec((1, 2 * HD, qb), lambda h, j: (h, 0, j)),
            by_q, whole, whole, pl.BlockSpec((HD, dqf.shape[1]), lambda h, j: (h, 0)),
        ],
        [by_q, whole, whole],
        [SDS((rows, tok), BF), SDS((rows, tok), F32), SDS((rows, tok), F32)],
        scratch=[pltpu.VMEM((tok, 2 * HD), BF)],
        flops=8 * rows * tok * tok, nbytes=2 * heads * tok * tok,
    )(offs, e, dob, q, k, v, dqf)


def merge(rate, offs, dk, dv, far):
    rows, tok = dk.shape
    return call(
        lambda *r: merge_kernel(rate, *r), "merge", (), [SMEM] + [WHOLE] * 3, [WHOLE] * 2,
        [SDS((rows, tok), BF)] * 2,
        flops=8 * rows * tok * far.shape[2], nbytes=12 * rows * tok,
    )(offs, dk, dv, far)


def shards(queries, keys, values, cotangent, w_out, lengths, offsets):
    rows, tok = queries.shape[1:]
    seq_count = lax.axis_size("seq")
    rate = tok * seq_count // SEL
    picks = tok // rate
    info = jnp.stack([lengths[0], lax.axis_index("seq").astype(jnp.int32) * tok])
    q, k, v = queries[0], keys[0], values[0]
    cot = lax.all_gather(cotangent[0], "head", axis=0, tiled=True)
    qp, kvp = pick(rate, offsets, q, k, v, picks)
    kvf = lax.all_gather(kvp, "seq")
    e, out_a, stats = forward(info, q, k, v)
    terms, attn, shares, out_b, pf = mid_a(rate, info, offsets, qp, kvf, out_a, stats, w_out)
    mixed = lax.psum_scatter(terms, "head", scatter_dimension=0, tiled=True)
    dob, dkv, dqf, wpart = mid_b(
        rate, info, offsets, cot, w_out, attn, shares, out_a, stats, out_b, pf, qp, kvf
    )
    far = lax.all_to_all(dkv, "seq", 0, 0)
    grad_scale = 1.0 / math.sqrt(tok * seq_count * lax.axis_size("dp"))
    pieces = wpart.astype(BF).reshape(seq_count, rows // seq_count, w_out.shape[1])
    mine = jnp.sum(lax.all_to_all(pieces, "seq", 0, 0).astype(F32), axis=0)
    mine = lax.psum(mine, "dp") * grad_scale
    weight_grad = lax.all_gather(mine, "seq", axis=0, tiled=True)
    dq, dk, dv = backward(rate, offsets, e, dob, q, k, v, dqf)
    kg, vg = merge(rate, offsets, dk, dv, far)
    return (mixed[None], dq[None], kg[None], vg[None], weight_grad)


def solution(mesh):
    full = P("dp", "head", "seq")
    return jax.shard_map(
        shards,
        mesh=mesh,
        in_specs=(full, full, full, full, P("head", None), P("dp"), P("head")),
        out_specs=(full, full, full, full, P("head", None)),
        check_vma=False,
    )
```

```python
import math

import jax
import jax.numpy as jnp
from jax import lax
from jax.experimental import pallas as pl
from jax.experimental.pallas import tpu as pltpu
from jax.sharding import PartitionSpec as P

SEL = 2048
HD = 64
NEGATIVE = -1e30
BF = jnp.bfloat16
F32 = jnp.float32
QB = 1024
CK = 512
SAFE = 2.0**40
VMEM_BYTES = 60 * 2**20


def dot(a, b, ca, cb):
    return lax.dot_general(a, b, (((ca,), (cb,)), ((), ())), preferred_element_type=F32)


def split2(x):
    hi = x.astype(BF)
    return hi, (x - hi.astype(F32)).astype(BF)


def split3(x):
    hi = x.astype(BF)
    rest = x - hi.astype(F32)
    mid = rest.astype(BF)
    return hi, mid, (rest - mid.astype(F32)).astype(BF)


def call(kern, name, grid, in_specs, out_specs, out_shape, scratch=(), us=1):
    return pl.pallas_call(
        kern,
        name=name,
        grid=grid,
        in_specs=in_specs,
        out_specs=out_specs,
        out_shape=out_shape,
        scratch_shapes=list(scratch),
        compiler_params=pltpu.CompilerParams(vmem_limit_bytes=VMEM_BYTES),
        cost_estimate=work(us),
    )


def work(us):
    return pl.CostEstimate(flops=int(us * 1.15e9), bytes_accessed=0, transcendentals=0)


SMEM = pl.BlockSpec(memory_space=pltpu.SMEM)
WHOLE = pl.BlockSpec(memory_space=pltpu.VMEM)


def sel_matrix(off, rate, rows, cols):
    pos = lax.broadcasted_iota(jnp.int32, (rows, cols), 0)
    num = lax.broadcasted_iota(jnp.int32, (rows, cols), 1)
    return jnp.where(pos == num * rate + off, 1.0, 0.0).astype(BF)


def place_matrix(off, rate, start, rows, cols):
    num = lax.broadcasted_iota(jnp.int32, (rows, cols), 0)
    pos = lax.broadcasted_iota(jnp.int32, (rows, cols), 1) + start
    return jnp.where(pos == num * rate + off, 1.0, 0.0).astype(BF)


def pick_kernel(rate, offs, q, k, v, qp, kvp):
    sel = sel_matrix(offs[pl.program_id(0)], rate, q.shape[1], qp.shape[1])
    got = dot(jnp.concatenate([q[...], k[...], v[...]], axis=0), sel, 1, 0).astype(BF)
    qp[...] = got[:HD]
    kvp[0] = got[HD : 2 * HD]
    kvp[1] = got[2 * HD :]


def stack_rows(count, parts):
    row = lax.broadcasted_iota(jnp.int32, (count, parts[0].shape[1]), 0)
    out = jnp.zeros(row.shape, F32)
    for i, part in enumerate(parts):
        out = jnp.where(row == i, part.astype(F32), out)
    return out.astype(BF)


def fwd_kernel(info, q, k, v, e_out, out, stats, kt, qa, va):
    tok = k.shape[1]
    qb = out.shape[1]
    step = pl.program_id(1)

    @pl.when(step == 0)
    def _():
        pos = lax.broadcasted_iota(jnp.int32, (HD, tok), 1) + info[1]
        row = lax.broadcasted_iota(jnp.int32, (HD, tok), 0)
        bias = jnp.where(
            row == 0, jnp.where(pos >= info[0], NEGATIVE, 0.0), jnp.where(row == 1, -1.0, 0.0)
        )
        kt[...] = jnp.concatenate([k[...], bias.astype(BF)], axis=0).T
        one = jnp.where(row == 0, 1.0, 0.0).astype(BF)
        qa[...] = jnp.concatenate([q[...] * jnp.asarray(0.125, BF), one], axis=0)
        first = dot(kt[:256, :], qa[...], 1, 0)
        top = jnp.max(jnp.max(first.reshape(32, 8, tok), axis=0), axis=0, keepdims=True)
        qa[HD:, :] = jnp.where(row == 0, 1.0, jnp.where(row == 1, top, 0.0)).astype(BF)
        row16 = lax.broadcasted_iota(jnp.int32, (16, tok), 0)
        va[...] = jnp.concatenate([v[...], jnp.where(row16 == 0, 1.0, 0.0).astype(BF)], axis=0)

    base = pl.multiple_of(step * qb, qb)

    def finish(cols, acc):
        rt = 1.0 / acc[HD : HD + 1]
        out[:, cols] = acc[:HD] * rt
        stats[0, :, cols] = jnp.broadcast_to(rt, (8, rt.shape[1]))

    qc = qa[:, pl.ds(base, qb)]
    for i in range(0, tok, CK):
        e_out[0, i : i + CK, :] = jnp.exp(dot(kt[i : i + CK, :], qc, 1, 0)).astype(BF)
    acc = dot(va[...], e_out[0], 1, 0)
    finish(slice(0, qb), acc)
    total = acc[HD : HD + 1]
    unsafe = jnp.max(jnp.where(total < SAFE, 0.0, 1.0)) > 0.0

    @pl.when(unsafe)
    def _():
        width = 128

        def redo(n, carry):
            c0 = pl.multiple_of(n * width, width)
            cols = pl.ds(c0, width)
            s = dot(kt[...], qa[:, pl.ds(pl.multiple_of(base + c0, width), width)], 1, 0)
            s = s - jnp.max(s, axis=0, keepdims=True)
            e_out[0, :, cols] = jnp.exp(s).astype(BF)
            finish(cols, dot(va[...], e_out[0, :, cols], 1, 0))
            return carry

        lax.fori_loop(0, qb // width, redo, 0)


def projg_kernel(rate, info, offs, c0, c1, c2, c3, w, out_a, stats, g_out, dob, cot):
    part, cols = c0.shape
    count = cot.shape[0] // part
    for s, block in enumerate((c0, c1, c2, c3)):
        owner = lax.rem(info[2] + (count - s), count)
        cot[pl.ds(pl.multiple_of(owner * part, part), part), :] = block[...]
    heads = stats.shape[0]
    here = lax.broadcasted_iota(jnp.int32, (1, cols), 1) + pl.program_id(0) * cols
    keep = jnp.where(here + info[1] < info[0], 1.0, 0.0)
    g_all = dot(w[...], cot[...], 1, 0).astype(BF).astype(F32) * keep
    g_out[...] = g_all.astype(BF)
    for h in range(heads):
        rows = slice(h * HD, (h + 1) * HD)
        g = jnp.where((here % rate) == offs[h], 0.0, g_all[rows])
        rt = stats[h, 0:1, :]
        delta = jnp.sum(g * out_a[rows, :], axis=0, keepdims=True)
        c_hi, c_lo = split2(-delta * rt)
        dob[h] = jnp.concatenate([(g * rt).astype(BF), stack_rows(HD, [c_hi, c_lo])], axis=0)


def softmax_rows(s):
    m = jnp.max(s, axis=1, keepdims=True)
    e = jnp.exp(s - m)
    t = jnp.sum(e, axis=1, keepdims=True)
    return (e * (1.0 / t)).astype(BF), m + jnp.log(t)


def far_parts(kv_own, kv_oth, rows):
    both = [ref.at[c] for ref in (kv_own, kv_oth) for c in range(ref.shape[0])]
    return tuple(jnp.concatenate([ref[n, rows, :] for ref in both], axis=1) for n in range(2))


def mida_kernel(
    rate, info, offs, qp, kv_own, kv_oth, k, v, out_a, w,
    t0, t1, t2, t3, attn, pa, pb, oa_p, ob_p, sh_p, wt,
):
    part = t0.shape[0]
    count = wt.shape[0] // part
    heads = pa.shape[0]
    tok = out_a.shape[1]
    picks = qp.shape[1]
    chips = kv_own.shape[0]
    length, start, core = info[0], info[1], info[3]
    here = lax.broadcasted_iota(jnp.int32, (1, tok), 1)
    keep = jnp.where(here + start < length, 1.0, 0.0)
    num = lax.broadcasted_iota(jnp.int32, (1, 2 * chips * picks), 1)
    chunk = num // picks
    rank = 2 * (chunk % chips) + jnp.where(chunk < chips, core, 1 - core)
    far_pos = (rank * picks + num % picks) * rate
    pick_pos = lax.broadcasted_iota(jnp.int32, (picks, 1), 0) * rate + start
    wt[...] = w[...].T
    for h in range(heads):
        rows = slice(h * HD, (h + 1) * HD)
        off = offs[h]
        kf, vf = far_parts(kv_own, kv_oth, rows)
        qs = qp[rows, :] * jnp.asarray(0.125, BF)
        p_b, lse_b = softmax_rows(
            jnp.where(far_pos + off < length, dot(qs, kf, 0, 0), NEGATIVE)
        )
        p_a, lse_a = softmax_rows(
            jnp.where(here + start < length, dot(qs, k[rows, :], 0, 0), NEGATIVE)
        )
        pa[h] = p_a
        pb[h] = p_b
        o_b = dot(p_b, vf, 1, 1)
        o_a = dot(p_a, v[rows, :], 1, 1)
        oa_p[h] = o_a
        ob_p[h] = o_b
        gap = lse_a - lse_b
        near = 1.0 / (1.0 + jnp.exp(-gap))
        far = 1.0 / (1.0 + jnp.exp(gap))
        sh_p[h] = jnp.concatenate(
            [jnp.broadcast_to(near, (picks, HD)), jnp.broadcast_to(far, (picks, HD))], axis=1
        )
        live = jnp.where(pick_pos + off < length, 1.0, 0.0)
        mixed_p = ((near * o_a + far * o_b) * live).astype(BF)
        spread = dot(mixed_p, place_matrix(off, rate, 0, picks, tok), 0, 0)
        attn[rows, :] = jnp.where((here % rate) == off, spread, out_a[rows, :] * keep).astype(BF)
    for s, term in enumerate((t0, t1, t2, t3)):
        owner = lax.rem(info[2] + s, count)
        out_rows = pl.ds(pl.multiple_of(owner * part, part), part)
        term[...] = dot(wt[out_rows, :], attn[...], 1, 0).astype(BF)


def midb_kernel(
    rate, info, offs, g_in, sh_p, oa_p, ob_p, pa, pb, qp, kv_own, kv_oth, k, v, attn,
    c0, c1, c2, c3, kept, sent, dqp, dkp, dvp, cot, sems,
):
    part = c0.shape[0]
    count = cot.shape[0] // part
    copies = []
    for s, block in enumerate((c0, c1, c2, c3)):
        owner = lax.rem(info[2] + (count - s), count)
        there = cot.at[pl.ds(pl.multiple_of(owner * part, part), part), :]
        copies.append(pltpu.make_async_copy(block, there, sems.at[s]))
        copies[-1].start()
    heads = pa.shape[0]
    tok = g_in.shape[1]
    picks = qp.shape[1]
    chips = kept.shape[0]
    width = heads * HD
    for h in range(heads):
        rows = slice(h * HD, (h + 1) * HD)
        g = dot(sel_matrix(offs[h], rate, tok, picks), g_in[rows, :], 0, 1)
        near, far = sh_p[h, :, :HD], sh_p[h, :, HD:]
        o_a, o_b = oa_p[h], ob_p[h]
        dlse = (near * far)[:, :1] * jnp.sum(g * (o_a - o_b), axis=1, keepdims=True)
        kf, vf = far_parts(kv_own, kv_oth, rows)
        q = qp[rows, :]

        def back(k_all, v_all, p, do, out, dl):
            delta = jnp.sum(do.astype(F32) * out, axis=1, keepdims=True)
            dp = dot(do, v_all, 1, 0) + (dl - delta)
            ds = (p.astype(F32) * dp * 0.125).astype(BF)
            return dot(ds, k_all, 1, 1), dot(q, ds, 1, 0), dot(do, p, 0, 0)

        dq_a, dk_a, dv_a = back(k[rows, :], v[rows, :], pa[h], (near * g).astype(BF), o_a, dlse)
        dq_b, dk_b, dv_b = back(kf, vf, pb[h], (far * g).astype(BF), o_b, -dlse)
        dqp[h] = (dq_a + dq_b).astype(BF)
        dkp[rows, :] = dk_a.astype(BF)
        dvp[rows, :] = dv_a.astype(BF)
        for n, grad in enumerate((dk_b.astype(BF), dv_b.astype(BF))):
            first = n * width + h * HD
            for i, ref in enumerate((kept, sent)):
                for c in range(chips):
                    cols = slice((i * chips + c) * picks, (i * chips + c + 1) * picks)
                    ref[c, first : first + HD, :] = grad[:, cols]
    for copy in copies:
        copy.wait()
    grad = dot(attn[...], cot[...], 1, 1)
    size = grad.shape[0] // (2 * chips)
    blank = jnp.zeros((16 - size, grad.shape[1]), F32)
    for side in range(2):

        @pl.when(info[3] == side)
        def _():
            for ref, core in ((kept, side), (sent, 1 - side)):
                for c in range(chips):
                    r = 2 * c + core
                    piece = jnp.concatenate([grad[r * size : (r + 1) * size], blank], axis=0)
                    piece = piece.astype(BF)
                    for n in range(grad.shape[1] // picks):
                        first = 2 * width + 16 * n
                        ref[c, first : first + 16, :] = piece[:, n * picks : (n + 1) * picks]


def bwd_kernel(e, dob, q, k, v, *rest):
    dq, dk, dv, vt = rest[-4:]
    tok = k.shape[1]
    qb = q.shape[1]
    step = pl.program_id(1)

    @pl.when(step == 0)
    def _():
        row = lax.broadcasted_iota(jnp.int32, (HD, tok), 0)
        ones = jnp.where(row < 2, 1.0, 0.0).astype(BF)
        vt[...] = jnp.concatenate([v[...], ones], axis=0).T
        dk[...] = jnp.zeros_like(dk)
        dv[...] = jnp.zeros_like(dv)

    ck = CK
    do = dob[0, :HD, :]
    acc = None
    for i in range(0, tok, ck):
        dp = dot(vt[i : i + ck, :], dob[0], 1, 0)
        ei = e[0, i : i + ck, :]
        ds = (ei.astype(F32) * dp).astype(BF)
        part = dot(k[:, i : i + ck], ds, 1, 0)
        acc = part if acc is None else acc + part
        dk[:, i : i + ck] += dot(q[...], ds, 1, 1)
        dv[:, i : i + ck] += dot(do, ei, 1, 1)
    dq[...] = (acc * 0.125).astype(BF)


def merge_kernel(rate, offs, dq, dk, dv, dqp, dkp, dvp, far_k, far_v, qg, kg, vg):
    place = place_matrix(offs[pl.program_id(0)], rate, 0, far_k.shape[2], dk.shape[1])
    sums = []
    for parts in (far_k, far_v):
        total = parts[0].astype(F32)
        for r in range(1, parts.shape[0]):
            total = total + parts[r].astype(F32)
        sums.append(total.astype(BF))
    spread = dot(jnp.concatenate(sums + [dqp[0].T], axis=0), place, 1, 0)
    near_k = dk[...] * 0.125 + dkp[...].astype(F32)
    near_v = dv[...] + dvp[...].astype(F32)
    kg[...] = (near_k + spread[:HD]).astype(BF)
    vg[...] = (near_v + spread[HD : 2 * HD]).astype(BF)
    qg[...] = (dq[...].astype(F32) + spread[2 * HD :]).astype(BF)


SDS = jax.ShapeDtypeStruct


def pick(rate, offs, q, k, v, picks):
    rows, tok = q.shape
    by_head = pl.BlockSpec((HD, tok), lambda h: (h, 0))
    return call(
        lambda *r: pick_kernel(rate, *r), "pick", (rows // HD,),
        [SMEM, by_head, by_head, by_head],
        [
            pl.BlockSpec((HD, picks), lambda h: (h, 0)),
            pl.BlockSpec((2, HD, picks), lambda h: (0, h, 0)),
        ],
        [SDS((rows, picks), BF), SDS((2, rows, picks), BF)],
        us=2,
    )(offs, q, k, v)


def forward(info, q, k, v):
    rows, tok = q.shape
    heads = rows // HD
    qb = min(QB, tok)
    by_q = pl.BlockSpec((HD, qb), lambda h, j: (h, j))
    whole = pl.BlockSpec((HD, tok), lambda h, j: (h, 0))
    return call(
        fwd_kernel, "fwd", (heads, tok // qb), [SMEM, whole, whole, whole],
        [
            pl.BlockSpec((1, tok, qb), lambda h, j: (h, 0, j)),
            by_q,
            pl.BlockSpec((1, 8, qb), lambda h, j: (h, 0, j)),
        ],
        [SDS((heads, tok, tok), BF), SDS((rows, tok), F32), SDS((heads, 8, tok), F32)],
        scratch=[
            pltpu.VMEM((tok, 2 * HD), BF), pltpu.VMEM((2 * HD, tok), BF),
            pltpu.VMEM((HD + 16, tok), BF),
        ],
        us=18,
    )(info, q, k, v)


def project(rate, info, offs, blocks, w, out_a, stats):
    rows, tok = out_a.shape
    heads = rows // HD
    cols = tok // 4
    by_p = pl.BlockSpec((rows, cols), lambda j: (0, j))
    by_h = lambda n: pl.BlockSpec((heads, n, cols), lambda j: (0, 0, j))
    return call(
        lambda *r: projg_kernel(rate, *r), "projg", (tok // cols,),
        [SMEM, SMEM] + [by_p] * 4 + [WHOLE, by_p, by_h(8)],
        [by_p, by_h(2 * HD)],
        [SDS((rows, tok), BF), SDS((heads, 2 * HD, tok), BF)],
        scratch=[pltpu.VMEM((w.shape[1], cols), BF)],
        us=4,
    )(info, offs, *blocks, w, out_a, stats)


def mid_a(rate, info, offs, qp, kv_own, kv_oth, k, v, out_a, w):
    rows, tok = out_a.shape
    heads = rows // HD
    picks = qp.shape[1]
    far = 2 * kv_own.shape[0] * picks
    return call(
        lambda *r: mida_kernel(rate, *r), "mida", (), [SMEM, SMEM] + [WHOLE] * 7, [WHOLE] * 10,
        [SDS((rows, tok), BF)] * 5
        + [
            SDS((heads, picks, tok), BF), SDS((heads, picks, far), BF),
            SDS((heads, picks, HD), F32), SDS((heads, picks, HD), F32),
            SDS((heads, picks, 2 * HD), F32),
        ],
        scratch=[pltpu.VMEM((w.shape[1], rows), BF)],
        us=10,
    )(info, offs, qp, kv_own, kv_oth, k, v, out_a, w)


def mid_b(rate, info, offs, g, sh_p, oa_p, ob_p, pa, pb, qp, kv_own, kv_oth, k, v, attn, blocks):
    rows, tok = g.shape
    heads = rows // HD
    picks = qp.shape[1]
    count = len(blocks)
    chips = kv_own.shape[0]
    anywhere = pl.BlockSpec(memory_space=pl.ANY)
    half = SDS((chips, 2 * rows + 16 * (count * rows // picks), picks), BF)
    return call(
        lambda *r: midb_kernel(rate, *r), "midb", (),
        [SMEM, SMEM] + [WHOLE] * 12 + [anywhere] * 4, [WHOLE] * 5,
        [half, half, SDS((heads, picks, HD), BF), SDS((rows, tok), BF), SDS((rows, tok), BF)],
        scratch=[pltpu.VMEM((count * rows, tok), BF), pltpu.SemaphoreType.DMA((count,))],
        us=10,
    )(info, offs, g, sh_p, oa_p, ob_p, pa, pb, qp, kv_own, kv_oth, k, v, attn, *blocks)


def hold(x, after):
    anywhere = pl.BlockSpec(memory_space=pl.ANY)
    return pl.pallas_call(
        lambda *refs: None, name="hold", in_specs=[anywhere] * 2, out_specs=anywhere,
        out_shape=SDS(x.shape, x.dtype), input_output_aliases={0: 0},
    )(x, after)


def total_kernel(parts, after, out):
    total = parts[0].astype(F32)
    for r in range(1, parts.shape[0]):
        total = total + parts[r].astype(F32)
    out[...] = total


def total(parts, first, after):
    count, rows, cols = parts.shape
    rows -= first
    return call(
        total_kernel, "total", (1,),
        [
            pl.BlockSpec((count, rows, cols), lambda i: (0, first // rows, 0)),
            pl.BlockSpec(memory_space=pl.ANY),
        ],
        pl.BlockSpec((rows, cols), lambda i: (0, 0)),
        SDS((rows, cols), F32), us=1,
    )(parts, after)


def backward(first, heads, e, dob, q, k, v, earlier, after):
    rows, tok = q.shape
    qb = min(QB, tok)
    by_q = pl.BlockSpec((HD, qb), lambda h, j: (first + h, j))
    whole = pl.BlockSpec((HD, tok), lambda h, j: (first + h, 0))
    anywhere = pl.BlockSpec(memory_space=pl.ANY)
    n_in = 5 + len(after)
    return pl.pallas_call(
        bwd_kernel,
        name="bwd%d" % first,
        grid=(heads, tok // qb),
        in_specs=[
            pl.BlockSpec((1, tok, qb), lambda h, j: (first + h, 0, j)),
            pl.BlockSpec((1, 2 * HD, qb), lambda h, j: (first + h, 0, j)),
            by_q, whole, whole,
        ]
        + [anywhere] * (len(after) + len(earlier)),
        out_specs=[by_q, whole, whole],
        out_shape=[SDS((rows, tok), BF), SDS((rows, tok), F32), SDS((rows, tok), F32)],
        scratch_shapes=[pltpu.VMEM((tok, 2 * HD), BF)],
        input_output_aliases={n_in + i: i for i in range(len(earlier))},
        compiler_params=pltpu.CompilerParams(vmem_limit_bytes=VMEM_BYTES),
        cost_estimate=work(12 * heads),
    )(e, dob, q, k, v, *after, *earlier)


def merge(rate, offs, dq, dk, dv, dqp, dkp, dvp, far):
    rows, tok = dk.shape
    heads = rows // HD
    chips, _, picks = far.shape
    by_head = pl.BlockSpec((HD, tok), lambda h: (h, 0))
    return call(
        lambda *r: merge_kernel(rate, *r), "merge", (heads,),
        [SMEM] + [by_head] * 3 + [pl.BlockSpec((1, picks, HD), lambda h: (h, 0, 0))]
        + [by_head] * 2
        + [
            pl.BlockSpec((chips, HD, picks), lambda h: (0, h, 0)),
            pl.BlockSpec((chips, HD, picks), lambda h: (0, heads + h, 0)),
        ],
        [by_head] * 3,
        [SDS((rows, tok), BF)] * 3,
        us=5,
    )(offs, dq, dk, dv, dqp, dkp, dvp, far, far)


def shift(x, axis, by):
    count = lax.axis_size(axis)
    return lax.ppermute(x, axis, [(i, (i + by) % count) for i in range(count)])


def shards(queries, keys, values, cotangent, w_out, lengths, offsets):
    rows, tok = queries.shape[1:]
    seq_count = lax.axis_size("seq")
    rate = tok * seq_count // SEL
    picks = tok // rate
    place = lax.axis_index("seq").astype(jnp.int32)
    info = jnp.stack(
        [
            lengths[0], place * tok, lax.axis_index("head").astype(jnp.int32), place % 2,
            place // 2,
        ]
    )
    q, k, v = queries[0], keys[0], values[0]
    groups = [list(range(c, seq_count, 2)) for c in range(2)]
    chips = seq_count // 2
    swap = [(i, i ^ 1) for i in range(seq_count)]
    qp, kvp = pick(rate, offsets, q, k, v, picks)
    kv_own = lax.all_to_all(
        jnp.broadcast_to(kvp[None], (chips,) + kvp.shape), "seq", 0, 0, axis_index_groups=groups
    )
    own = cotangent[0]
    blocks = [own] + [shift(own, "head", s) for s in (1, 2, 3)]
    e, out_a, stats = forward(info, q, k, v)
    kv_own = hold(kv_own, stats)
    kv_oth = lax.ppermute(kv_own, "seq", swap)
    *terms, attn, pa, pb, oa_p, ob_p, sh_p = mid_a(
        rate, info, offsets, qp, kv_own, kv_oth, k, v, out_a, w_out
    )
    sent_terms = [shift(terms[s], "head", s) for s in (1, 2, 3)]
    g, dob = project(rate, info, offsets, blocks, w_out, out_a, stats)
    kept, sent, dqp, dkp, dvp = mid_b(
        rate, info, offsets, g, sh_p, oa_p, ob_p, pa, pb, qp, kv_own, kv_oth, k, v, attn, blocks
    )
    got = lax.ppermute(sent, "seq", swap)
    pair = (kept.astype(F32) + got.astype(F32)).astype(BF)
    far = lax.all_to_all(pair, "seq", 0, 0, axis_index_groups=groups)
    grads = backward(0, 2, e, dob, q, k, v, (), (pair,))
    mine = total(far, 2 * rows, grads[0]).reshape(-1, 16, picks)[:, : rows // seq_count]
    mine = mine.transpose(1, 0, 2).reshape(rows // seq_count, -1)
    grad_scale = 1.0 / math.sqrt(tok * seq_count * lax.axis_size("dp"))
    mine = (mine + sum(shift(mine, "dp", s) for s in (1, 2, 3))) * grad_scale
    weight_grad = lax.all_to_all(
        jnp.broadcast_to(mine[None], (seq_count,) + mine.shape), "seq", 0, 0
    ).reshape(w_out.shape)
    dq, dk, dv = backward(2, 1, e, dob, q, k, v, grads, sent_terms)
    mixed = sum(t.astype(F32) for t in [terms[0]] + sent_terms).astype(BF)
    qg, kg, vg = merge(rate, offsets, dq, dk, dv, dqp, dkp, dvp, far)
    return (mixed[None], qg[None], kg[None], vg[None], weight_grad)


def solution(mesh):
    full = P("dp", "head", "seq")
    return jax.shard_map(
        shards,
        mesh=mesh,
        in_specs=(full, full, full, full, P("head", None), P("dp"), P("head")),
        out_specs=(full, full, full, full, P("head", None)),
        check_vma=False,
    )
```

```python
import math

import jax
import jax.numpy as jnp
from jax import lax
from jax.experimental import pallas as pl
from jax.experimental.pallas import tpu as pltpu
from jax.sharding import PartitionSpec as P

SEL = 2048
HD = 64
NEGATIVE = -1e30
BF = jnp.bfloat16
F32 = jnp.float32
QB = 1024
CK = 512
SAFE = 2.0**40
VMEM_BYTES = 60 * 2**20


def dot(a, b, ca, cb):
    return lax.dot_general(a, b, (((ca,), (cb,)), ((), ())), preferred_element_type=F32)


def split2(x):
    hi = x.astype(BF)
    return hi, (x - hi.astype(F32)).astype(BF)


def split3(x):
    hi = x.astype(BF)
    rest = x - hi.astype(F32)
    mid = rest.astype(BF)
    return hi, mid, (rest - mid.astype(F32)).astype(BF)


def call(kern, name, grid, in_specs, out_specs, out_shape, scratch=(), us=1):
    return pl.pallas_call(
        kern,
        name=name,
        grid=grid,
        in_specs=in_specs,
        out_specs=out_specs,
        out_shape=out_shape,
        scratch_shapes=list(scratch),
        compiler_params=pltpu.CompilerParams(vmem_limit_bytes=VMEM_BYTES),
        cost_estimate=work(us),
    )


def work(us):
    return pl.CostEstimate(flops=int(us * 1.15e9), bytes_accessed=0, transcendentals=0)


SMEM = pl.BlockSpec(memory_space=pltpu.SMEM)
WHOLE = pl.BlockSpec(memory_space=pltpu.VMEM)


def sel_matrix(off, rate, rows, cols):
    pos = lax.broadcasted_iota(jnp.int32, (rows, cols), 0)
    num = lax.broadcasted_iota(jnp.int32, (rows, cols), 1)
    return jnp.where(pos == num * rate + off, 1.0, 0.0).astype(BF)


def place_matrix(off, rate, start, rows, cols):
    num = lax.broadcasted_iota(jnp.int32, (rows, cols), 0)
    pos = lax.broadcasted_iota(jnp.int32, (rows, cols), 1) + start
    return jnp.where(pos == num * rate + off, 1.0, 0.0).astype(BF)


def pick_kernel(rate, offs, q, k, v, qp, kvp):
    sel = sel_matrix(offs[pl.program_id(0)], rate, q.shape[1], qp.shape[1])
    got = dot(jnp.concatenate([q[...], k[...], v[...]], axis=0), sel, 1, 0).astype(BF)
    qp[...] = got[:HD]
    for c in range(kvp.shape[0]):
        kvp[c, 0] = got[HD : 2 * HD]
        kvp[c, 1] = got[2 * HD :]


def stack_rows(count, parts):
    row = lax.broadcasted_iota(jnp.int32, (count, parts[0].shape[1]), 0)
    out = jnp.zeros(row.shape, F32)
    for i, part in enumerate(parts):
        out = jnp.where(row == i, part.astype(F32), out)
    return out.astype(BF)


def fwd_kernel(info, q, k, v, qp, e_out, out, stats, pa, oa_p, lse_p, kt, qa, va):
    tok = k.shape[1]
    qb = out.shape[1]
    step = pl.program_id(1)

    @pl.when(step == 0)
    def _():
        pos = lax.broadcasted_iota(jnp.int32, (HD, tok), 1) + info[1]
        row = lax.broadcasted_iota(jnp.int32, (HD, tok), 0)
        bias = jnp.where(
            row == 0, jnp.where(pos >= info[0], NEGATIVE, 0.0), jnp.where(row == 1, -1.0, 0.0)
        )
        kt[...] = jnp.concatenate([k[...], bias.astype(BF)], axis=0).T
        one = jnp.where(row == 0, 1.0, 0.0).astype(BF)
        qa[...] = jnp.concatenate([q[...] * jnp.asarray(0.125, BF), one], axis=0)
        first = dot(kt[:256, :], qa[...], 1, 0)
        top = jnp.max(jnp.max(first.reshape(32, 8, tok), axis=0), axis=0, keepdims=True)
        qa[HD:, :] = jnp.where(row == 0, 1.0, jnp.where(row == 1, top, 0.0)).astype(BF)
        row16 = lax.broadcasted_iota(jnp.int32, (16, tok), 0)
        va[...] = jnp.concatenate([v[...], jnp.where(row16 == 0, 1.0, 0.0).astype(BF)], axis=0)

    base = pl.multiple_of(step * qb, qb)

    def finish(cols, acc):
        rt = 1.0 / acc[HD : HD + 1]
        out[:, cols] = acc[:HD] * rt
        stats[0, :, cols] = jnp.broadcast_to(rt, (8, rt.shape[1]))

    qc = qa[:, pl.ds(base, qb)]
    for i in range(0, tok, CK):
        e_out[0, i : i + CK, :] = jnp.exp(dot(kt[i : i + CK, :], qc, 1, 0)).astype(BF)
    acc = dot(va[...], e_out[0], 1, 0)
    finish(slice(0, qb), acc)
    total = acc[HD : HD + 1]
    unsafe = jnp.max(jnp.where(total < SAFE, 0.0, 1.0)) > 0.0

    @pl.when(step == pl.num_programs(1) - 1)
    def _():
        qs = qp[...] * jnp.asarray(0.125, BF)
        here = lax.broadcasted_iota(jnp.int32, (1, tok), 1)
        s = jnp.where(here + info[1] < info[0], dot(qs, k[...], 0, 0), NEGATIVE)
        p, lse = softmax_rows(s)
        pa[0] = p
        oa_p[0] = dot(p, v[...], 1, 1)
        lse_p[0] = jnp.broadcast_to(lse, lse_p.shape[1:])

    @pl.when(unsafe)
    def _():
        width = 128

        def redo(n, carry):
            c0 = pl.multiple_of(n * width, width)
            cols = pl.ds(c0, width)
            s = dot(kt[...], qa[:, pl.ds(pl.multiple_of(base + c0, width), width)], 1, 0)
            s = s - jnp.max(s, axis=0, keepdims=True)
            e_out[0, :, cols] = jnp.exp(s).astype(BF)
            finish(cols, dot(va[...], e_out[0, :, cols], 1, 0))
            return carry

        lax.fori_loop(0, qb // width, redo, 0)


def softmax_rows(s):
    m = jnp.max(s, axis=1, keepdims=True)
    e = jnp.exp(s - m)
    t = jnp.sum(e, axis=1, keepdims=True)
    return (e * (1.0 / t)).astype(BF), m + jnp.log(t)


def far_parts(kv_own, kv_oth, rows):
    both = [ref.at[c] for ref in (kv_own, kv_oth) for c in range(ref.shape[0])]
    return tuple(jnp.concatenate([ref[n, rows, :] for ref in both], axis=1) for n in range(2))


def mid_kernel(
    rate, info, offs, qp, kv_own, kv_oth, k, v, stats, w, pa, oa_p, lse_p, out_a, c0, c1, c2, c3,
    t0, t1, t2, t3, dob, kept, sent, dqp, dkp, dvp,
    wt, attn, pb, g_buf, oa, cot, t_buf, dob_buf, in_sems, out_sems,
):
    part = c0.shape[0]
    count = cot.shape[0] // part
    heads = pa.shape[0]
    tok = attn.shape[1]
    picks = qp.shape[1]
    chips = kv_own.shape[0]
    width = heads * HD
    length, start, core = info[0], info[1], info[3]
    oa_copy = pltpu.make_async_copy(out_a, oa, in_sems.at[count])
    oa_copy.start()
    copies = []
    for s, block in enumerate((c0, c1, c2, c3)):
        owner = lax.rem(info[2] + (count - s), count)
        there = cot.at[pl.ds(pl.multiple_of(owner * part, part), part), :]
        copies.append(pltpu.make_async_copy(block, there, in_sems.at[s]))
        copies[-1].start()

    here = lax.broadcasted_iota(jnp.int32, (1, tok), 1)
    keep = jnp.where(here + start < length, 1.0, 0.0)
    num = lax.broadcasted_iota(jnp.int32, (1, 2 * chips * picks), 1)
    chunk = num // picks
    rank = 2 * (chunk % chips) + jnp.where(chunk < chips, core, 1 - core)
    far_pos = (rank * picks + num % picks) * rate
    pick_pos = lax.broadcasted_iota(jnp.int32, (picks, 1), 0) * rate + start
    wt[...] = w[...].T
    kept_parts = []
    mixed_parts = []
    for h in range(heads):
        rows = slice(h * HD, (h + 1) * HD)
        off = offs[h]
        kf, vf = far_parts(kv_own, kv_oth, rows)
        qs = qp[rows, :] * jnp.asarray(0.125, BF)
        p_b, lse_b = softmax_rows(
            jnp.where(far_pos + off < length, dot(qs, kf, 0, 0), NEGATIVE)
        )
        pb[h] = p_b
        o_b = dot(p_b, vf, 1, 1)
        o_a, lse_a = oa_p[h], lse_p[h, :, :1]
        gap = lse_a - lse_b
        near = 1.0 / (1.0 + jnp.exp(-gap))
        far = 1.0 / (1.0 + jnp.exp(gap))
        kept_parts.append((o_a, o_b, near, far))
        live = jnp.where(pick_pos + off < length, 1.0, 0.0)
        mixed_parts.append(((near * o_a + far * o_b) * live).astype(BF))
    oa_copy.wait()
    for h in range(heads):
        rows = slice(h * HD, (h + 1) * HD)
        spread = dot(mixed_parts[h], place_matrix(offs[h], rate, 0, picks, tok), 0, 0)
        attn[rows, :] = jnp.where(
            (here % rate) == offs[h], spread, oa[rows, :] * keep
        ).astype(BF)
    sends = []
    for s, term in enumerate((t0, t1, t2, t3)):
        owner = lax.rem(info[2] + s, count)
        out_rows = pl.ds(pl.multiple_of(owner * part, part), part)
        t_buf[s] = dot(wt[out_rows, :], attn[...], 1, 0).astype(BF)
        sends.append(pltpu.make_async_copy(t_buf.at[s], term, out_sems.at[s]))
        sends[-1].start()

    for copy in copies:
        copy.wait()
    for h in range(heads):
        rows = slice(h * HD, (h + 1) * HD)
        g_all = dot(w[rows, :], cot[...], 1, 0).astype(BF).astype(F32) * keep
        g_buf[rows, :] = g_all.astype(BF)
        g = jnp.where((here % rate) == offs[h], 0.0, g_all)
        rt = stats[h, 0:1, :]
        delta = jnp.sum(g * oa[rows, :], axis=0, keepdims=True)
        c_hi, c_lo = split2(-delta * rt)
        dob_buf[h] = jnp.concatenate(
            [(g * rt).astype(BF), stack_rows(HD, [c_hi, c_lo])], axis=0
        )
    sends.append(pltpu.make_async_copy(dob_buf, dob, out_sems.at[count]))
    sends[-1].start()

    for h in range(heads):
        rows = slice(h * HD, (h + 1) * HD)
        g = dot(sel_matrix(offs[h], rate, tok, picks), g_buf[rows, :], 0, 1)
        o_a, o_b, near, far = kept_parts[h]
        dlse = near * far * jnp.sum(g * (o_a - o_b), axis=1, keepdims=True)
        kf, vf = far_parts(kv_own, kv_oth, rows)
        q = qp[rows, :]

        def back(k_all, v_all, p, do, out, dl):
            delta = jnp.sum(do.astype(F32) * out, axis=1, keepdims=True)
            dp = dot(do, v_all, 1, 0) + (dl - delta)
            ds = (p.astype(F32) * dp * 0.125).astype(BF)
            return dot(ds, k_all, 1, 1), dot(q, ds, 1, 0), dot(do, p, 0, 0)

        dq_a, dk_a, dv_a = back(k[rows, :], v[rows, :], pa[h], (near * g).astype(BF), o_a, dlse)
        dq_b, dk_b, dv_b = back(kf, vf, pb[h], (far * g).astype(BF), o_b, -dlse)
        dqp[h] = (dq_a + dq_b).astype(BF)
        dkp[rows, :] = dk_a.astype(BF)
        dvp[rows, :] = dv_a.astype(BF)
        for n, grad in enumerate((dk_b.astype(BF), dv_b.astype(BF))):
            first = n * width + h * HD
            for i, ref in enumerate((kept, sent)):
                for c in range(chips):
                    cols = slice((i * chips + c) * picks, (i * chips + c + 1) * picks)
                    ref[c, first : first + HD, :] = grad[:, cols]
    grad = dot(attn[...], cot[...], 1, 1)
    size = grad.shape[0] // chips
    half = grad.shape[1] // 2
    blank = jnp.zeros((32 - size, picks), F32)
    for side in range(2):

        @pl.when(core == side)
        def _():
            for ref, parity in ((kept, side), (sent, 1 - side)):
                for c in range(chips):
                    for n in range(half // picks):
                        left = parity * half + n * picks
                        piece = grad[c * size : (c + 1) * size, left : left + picks]
                        first = 2 * width + 32 * n
                        ref[c, first : first + 32, :] = jnp.concatenate(
                            [piece, blank], axis=0
                        ).astype(BF)
    for send in sends:
        send.wait()


def bwd_step(rate, off, e, dob, q, k, v, dqp, dkp, dvp, dq, dk, dv, vt):
    tok = k.shape[1]
    qb = q.shape[1]
    step = pl.program_id(1)

    @pl.when(step == 0)
    def _():
        row = lax.broadcasted_iota(jnp.int32, (HD, tok), 0)
        ones = jnp.where(row < 2, 1.0, 0.0).astype(BF)
        vt[...] = jnp.concatenate([v[...], ones], axis=0).T
        dk[...] = dkp[...].astype(F32) * 8.0
        dv[...] = dvp[...].astype(F32)

    do = dob[0, :HD, :]
    acc = None
    for i in range(0, tok, CK):
        dp = dot(vt[i : i + CK, :], dob[0], 1, 0)
        ei = e[0, i : i + CK, :]
        ds = (ei.astype(F32) * dp).astype(BF)
        part = dot(k[:, i : i + CK], ds, 1, 0)
        acc = part if acc is None else acc + part
        dk[:, i : i + CK] += dot(q[...], ds, 1, 1)
        dv[:, i : i + CK] += dot(do, ei, 1, 1)
    place = place_matrix(off, rate, step * qb, dqp.shape[1], qb)
    dq[...] = (acc * 0.125 + dot(dqp[0], place, 0, 0)).astype(BF)


def bwd_kernel(rate, offs, e, dob, q, k, v, dqp, dkp, dvp, dq, dk, dv, vt):
    off = offs[pl.program_id(0)]
    bwd_step(rate, off, e, dob, q, k, v, dqp, dkp, dvp, dq, dk, dv, vt)


def far_sum(rate, off, far_k, far_v, tok):
    sums = []
    for parts in (far_k, far_v):
        total = parts[0].astype(F32)
        for r in range(1, parts.shape[0]):
            total = total + parts[r].astype(F32)
        sums.append(total.astype(BF))
    place = place_matrix(off, rate, 0, far_k.shape[2], tok)
    return dot(jnp.concatenate(sums, axis=0), place, 1, 0)


def last_kernel(
    rate, last, offs, e, dob, q, k, v, dqp, dkp, dvp, far_k, far_v,
    dk_old, dv_old, old_k, old_v, t0, t1, t2, t3, dq_old,
    dq, kg, vg, mixed, dk, dv, k_buf, v_buf, vt, sems,
):
    tok = k.shape[1]
    step = pl.program_id(1)
    bwd_step(rate, offs[last], e, dob, q, k, v, dqp, dkp, dvp, dq, dk, dv, vt)

    def store(slot, head, near_k, near_v, spread):
        k_buf[slot] = (near_k * 0.125 + spread[:HD]).astype(BF)
        v_buf[slot] = (near_v + spread[HD:]).astype(BF)
        rows = pl.ds(pl.multiple_of(head * HD, HD), HD)
        for n, (buf, out) in enumerate(((k_buf, kg), (v_buf, vg))):
            pltpu.make_async_copy(buf.at[slot], out.at[rows, :], sems.at[slot, n]).start()

    def wait(slot):
        for n, (buf, out) in enumerate(((k_buf, kg), (v_buf, vg))):
            pltpu.make_async_copy(buf.at[slot], out.at[:HD, :], sems.at[slot, n]).wait()

    store(step, step, dk_old[...], dv_old[...], far_sum(rate, offs[step], old_k, old_v, tok))
    total = t0[...].astype(F32)
    for t in (t1, t2, t3):
        total = total + t[...].astype(F32)
    mixed[...] = total.astype(BF)

    @pl.when(step == last - 1)
    def _():
        store(last, last, dk[...], dv[...], far_sum(rate, offs[last], far_k, far_v, tok))
        for slot in range(last + 1):
            wait(slot)


SDS = jax.ShapeDtypeStruct


def pick(rate, offs, q, k, v, picks, copies):
    rows, tok = q.shape
    by_head = pl.BlockSpec((HD, tok), lambda h: (h, 0))
    return call(
        lambda *r: pick_kernel(rate, *r), "pick", (rows // HD,),
        [SMEM, by_head, by_head, by_head],
        [
            pl.BlockSpec((HD, picks), lambda h: (h, 0)),
            pl.BlockSpec((copies, 2, HD, picks), lambda h: (0, 0, h, 0)),
        ],
        [SDS((rows, picks), BF), SDS((copies, 2, rows, picks), BF)],
        us=2,
    )(offs, q, k, v)


def forward(info, q, k, v, qp):
    rows, tok = q.shape
    heads = rows // HD
    picks = qp.shape[1]
    qb = min(QB, tok)
    by_q = pl.BlockSpec((HD, qb), lambda h, j: (h, j))
    whole = pl.BlockSpec((HD, tok), lambda h, j: (h, 0))
    by_h = lambda n: pl.BlockSpec((1, picks, n), lambda h, j: (h, 0, 0))
    return call(
        fwd_kernel, "fwd", (heads, tok // qb),
        [SMEM, whole, whole, whole, pl.BlockSpec((HD, picks), lambda h, j: (h, 0))],
        [
            pl.BlockSpec((1, tok, qb), lambda h, j: (h, 0, j)),
            by_q,
            pl.BlockSpec((1, 8, qb), lambda h, j: (h, 0, j)),
            by_h(tok), by_h(HD), by_h(HD),
        ],
        [
            SDS((heads, tok, tok), BF), SDS((rows, tok), F32), SDS((heads, 8, tok), F32),
            SDS((heads, picks, tok), BF), SDS((heads, picks, HD), F32),
            SDS((heads, picks, HD), F32),
        ],
        scratch=[
            pltpu.VMEM((tok, 2 * HD), BF), pltpu.VMEM((2 * HD, tok), BF),
            pltpu.VMEM((HD + 16, tok), BF),
        ],
        us=18,
    )(info, q, k, v, qp)


def middle(rate, info, offs, qp, kv_own, kv_oth, k, v, stats, w, near, out_a, blocks):
    rows, tok = k.shape
    heads = rows // HD
    picks = qp.shape[1]
    count = len(blocks)
    chips = kv_own.shape[0]
    far = 2 * chips * picks
    anywhere = pl.BlockSpec(memory_space=pl.ANY)
    half = SDS((chips, 2 * rows + 16 * (count * rows // picks), picks), BF)
    dob = (heads, 2 * HD, tok)
    return call(
        lambda *r: mid_kernel(rate, *r), "mid", (),
        [SMEM, SMEM] + [WHOLE] * 10 + [anywhere] * 5,
        [anywhere] * 5 + [WHOLE] * 5,
        [SDS((rows, tok), BF)] * count
        + [
            SDS(dob, BF), half, half, SDS((heads, picks, HD), BF), SDS((rows, tok), BF),
            SDS((rows, tok), BF),
        ],
        scratch=[
            pltpu.VMEM((count * rows, rows), BF), pltpu.VMEM((rows, tok), BF),
            pltpu.VMEM((heads, picks, far), BF),
            pltpu.VMEM((rows, tok), BF), pltpu.VMEM((rows, tok), F32),
            pltpu.VMEM((count * rows, tok), BF), pltpu.VMEM((count, rows, tok), BF),
            pltpu.VMEM(dob, BF), pltpu.SemaphoreType.DMA((count + 1,)),
            pltpu.SemaphoreType.DMA((count + 1,)),
        ],
        us=20,
    )(info, offs, qp, kv_own, kv_oth, k, v, stats, w, *near, out_a, *blocks)


def hold_all(arrays, after):
    anywhere = pl.BlockSpec(memory_space=pl.ANY)
    count = len(arrays)
    return pl.pallas_call(
        lambda *refs: None, name="hold", in_specs=[anywhere] * (count + 1),
        out_specs=[anywhere] * count, out_shape=[SDS(x.shape, x.dtype) for x in arrays],
        input_output_aliases={i: i for i in range(count)},
    )(*arrays, after)


def hold(x, after):
    return hold_all([x], after)[0]


def total_kernel(parts, after, out):
    total = parts[0].astype(F32)
    for r in range(1, parts.shape[0]):
        total = total + parts[r].astype(F32)
    cols = total.shape[1]
    mine = jnp.concatenate(
        [total[r : r + out.shape[1]] for r in range(0, total.shape[0], 32)], axis=1
    )
    for r in range(out.shape[0]):
        out[r] = mine


def total(parts, first, size, copies, after):
    count, rows, cols = parts.shape
    rows -= first
    shape = (copies, size, rows // 32 * cols)
    return call(
        total_kernel, "total", (1,),
        [
            pl.BlockSpec((count, rows, cols), lambda i: (0, first // rows, 0)),
            pl.BlockSpec(memory_space=pl.ANY),
        ],
        pl.BlockSpec(shape, lambda i: (0, 0, 0)),
        SDS(shape, F32), us=1,
    )(parts, after)


def spread_kernel(scale, parts, out):
    mine = parts[0]
    for r in range(1, parts.shape[0]):
        mine = mine + parts[r]
    mine = mine * scale
    for r in range(out.shape[0]):
        out[r] = mine


def spread_sum(scale, parts, copies):
    return call(
        lambda *r: spread_kernel(scale, *r), "spread", (), [WHOLE], WHOLE,
        SDS((copies,) + parts.shape[1:], F32), us=1,
    )(parts)


def backward_specs(first, rows, tok, picks):
    qb = min(QB, tok)
    by_q = pl.BlockSpec((HD, qb), lambda h, j: (first + h, j))
    whole = pl.BlockSpec((HD, tok), lambda h, j: (first + h, 0))
    ins = [
        SMEM,
        pl.BlockSpec((1, tok, qb), lambda h, j: (first + h, 0, j)),
        pl.BlockSpec((1, 2 * HD, qb), lambda h, j: (first + h, 0, j)),
        by_q, whole, whole, pl.BlockSpec((1, picks, HD), lambda h, j: (first + h, 0, 0)),
        whole, whole,
    ]
    return qb, by_q, whole, ins


def backward(heads, rate, offs, e, dob, q, k, v, dqp, dkp, dvp, after):
    rows, tok = q.shape
    qb, by_q, whole, ins = backward_specs(0, rows, tok, dqp.shape[1])
    spare = [pl.BlockSpec(memory_space=pl.ANY)] * len(after)

    def kernel(*refs):
        bwd_kernel(rate, *refs[:9], *refs[9 + len(after) :])

    return call(
        kernel, "bwd", (heads, tok // qb), ins + spare, [by_q, whole, whole],
        [SDS((rows, tok), BF)] + [SDS((heads * HD, tok), F32)] * 2,
        scratch=[pltpu.VMEM((tok, 2 * HD), BF)],
        us=11 * heads,
    )(offs, e, dob, q, k, v, dqp, dkp, dvp, *after)


def backward_last(rate, offs, e, dob, q, k, v, dqp, dkp, dvp, far, dq_old, dk_old, dv_old, terms):
    rows, tok = q.shape
    heads = rows // HD
    last = heads - 1
    chips, _, picks = far.shape
    qb, by_q, whole, ins = backward_specs(last, rows, tok, picks)
    assert tok // qb == last
    anywhere = pl.BlockSpec(memory_space=pl.ANY)
    of = lambda at: pl.BlockSpec((chips, HD, picks), lambda h, j: (0, at(j), 0))
    old = pl.BlockSpec((HD, tok), lambda h, j: (j, 0))
    slab = pl.BlockSpec((rows // last, tok), lambda h, j: (j, 0))
    ins = ins + [of(lambda j: last), of(lambda j: heads + last), old, old]
    ins = ins + [of(lambda j: j), of(lambda j: heads + j)] + [slab] * len(terms) + [anywhere]
    buf = pltpu.VMEM((heads, HD, tok), BF)
    return pl.pallas_call(
        lambda *r: last_kernel(rate, last, *r),
        name="last",
        grid=(1, tok // qb),
        in_specs=ins,
        out_specs=[by_q, anywhere, anywhere, slab],
        out_shape=[SDS((rows, tok), BF)] * 4,
        scratch_shapes=[
            pltpu.VMEM((HD, tok), F32), pltpu.VMEM((HD, tok), F32), buf, buf,
            pltpu.VMEM((tok, 2 * HD), BF), pltpu.SemaphoreType.DMA((heads, 2)),
        ],
        input_output_aliases={len(ins) - 1: 0},
        compiler_params=pltpu.CompilerParams(vmem_limit_bytes=VMEM_BYTES),
        cost_estimate=work(13),
    )(offs, e, dob, q, k, v, dqp, dkp, dvp, far, far, dk_old, dv_old, far, far, *terms, dq_old)


def shift(x, axis, by):
    count = lax.axis_size(axis)
    return lax.ppermute(x, axis, [(i, (i + by) % count) for i in range(count)])


def shards(queries, keys, values, cotangent, w_out, lengths, offsets):
    rows, tok = queries.shape[1:]
    seq_count = lax.axis_size("seq")
    rate = tok * seq_count // SEL
    picks = tok // rate
    place = lax.axis_index("seq").astype(jnp.int32)
    info = jnp.stack(
        [
            lengths[0], place * tok, lax.axis_index("head").astype(jnp.int32), place % 2,
            place // 2,
        ]
    )
    q, k, v = queries[0], keys[0], values[0]
    groups = [list(range(c, seq_count, 2)) for c in range(2)]
    chips = seq_count // 2
    swap = [(i, i ^ 1) for i in range(seq_count)]
    qp, kvp = pick(rate, offsets, q, k, v, picks, chips)
    kv_own = lax.all_to_all(kvp, "seq", 0, 0, axis_index_groups=groups)
    own = cotangent[0]
    blocks = [own] + [shift(own, "head", s) for s in (1, 2, 3)]
    e, out_a, stats, *near = forward(info, q, k, v, qp)
    kv_own = hold(kv_own, stats)
    kv_oth = lax.ppermute(kv_own, "seq", swap)
    *terms, dob, kept, sent, dqp, dkp, dvp = middle(
        rate, info, offsets, qp, kv_own, kv_oth, k, v, stats, w_out, near, out_a, blocks
    )
    got = lax.ppermute(sent, "seq", swap)
    pair = (kept.astype(F32) + got.astype(F32)).astype(BF)
    far = lax.all_to_all(pair, "seq", 0, 0, axis_index_groups=groups)
    later = hold_all(terms[1:], pair)
    terms = terms[:1] + [shift(t, "head", s + 1) for s, t in enumerate(later)]
    dq, dk, dv = backward(2, rate, offsets, e, dob, q, k, v, dqp, dkp, dvp, (pair,))
    grad_scale = 1.0 / math.sqrt(tok * seq_count * lax.axis_size("dp"))
    mine = total(far, 2 * rows, rows // chips, lax.axis_size("dp"), dk)
    mine = lax.all_to_all(mine, "dp", 0, 0)
    spread = lax.all_to_all(spread_sum(grad_scale, mine, seq_count), "seq", 0, 0)
    spread = spread.reshape((chips, 2) + spread.shape[1:])
    weight_grad = spread.transpose(0, 2, 1, 3).reshape(w_out.shape)
    dq, kg, vg, mixed = backward_last(
        rate, offsets, e, dob, q, k, v, dqp, dkp, dvp, far, dq, dk, dv, terms
    )
    return (mixed[None], dq[None], kg[None], vg[None], weight_grad)


def solution(mesh):
    full = P("dp", "head", "seq")
    return jax.shard_map(
        shards,
        mesh=mesh,
        in_specs=(full, full, full, full, P("head", None), P("dp"), P("head")),
        out_specs=(full, full, full, full, P("head", None)),
        check_vma=False,
    )
```

```python
import math

import jax
import jax.numpy as jnp
from jax import lax
from jax.experimental import pallas as pl
from jax.experimental.pallas import tpu as pltpu
from jax.sharding import PartitionSpec as P

SEL = 2048
HD = 64
NEGATIVE = -1e30
BF = jnp.bfloat16
F32 = jnp.float32
QB = 1024
CK = 512
SAFE = 2.0**40
VMEM_BYTES = 60 * 2**20


def dot(a, b, ca, cb):
    return lax.dot_general(a, b, (((ca,), (cb,)), ((), ())), preferred_element_type=F32)


def split2(x):
    hi = x.astype(BF)
    return hi, (x - hi.astype(F32)).astype(BF)


def split3(x):
    hi = x.astype(BF)
    rest = x - hi.astype(F32)
    mid = rest.astype(BF)
    return hi, mid, (rest - mid.astype(F32)).astype(BF)


def call(kern, name, grid, in_specs, out_specs, out_shape, scratch=(), us=1, mib=60):
    return pl.pallas_call(
        kern,
        name=name,
        grid=grid,
        in_specs=in_specs,
        out_specs=out_specs,
        out_shape=out_shape,
        scratch_shapes=list(scratch),
        compiler_params=pltpu.CompilerParams(vmem_limit_bytes=mib * 2**20),
        cost_estimate=work(us),
    )


def work(us):
    return pl.CostEstimate(flops=int(us * 1.15e9), bytes_accessed=0, transcendentals=0)


SMEM = pl.BlockSpec(memory_space=pltpu.SMEM)
WHOLE = pl.BlockSpec(memory_space=pltpu.VMEM)


def sel_matrix(off, rate, rows, cols):
    pos = lax.broadcasted_iota(jnp.int32, (rows, cols), 0)
    num = lax.broadcasted_iota(jnp.int32, (rows, cols), 1)
    return jnp.where(pos == num * rate + off, 1.0, 0.0).astype(BF)


def place_matrix(off, rate, start, rows, cols):
    num = lax.broadcasted_iota(jnp.int32, (rows, cols), 0)
    pos = lax.broadcasted_iota(jnp.int32, (rows, cols), 1) + start
    return jnp.where(pos == num * rate + off, 1.0, 0.0).astype(BF)


def pick_kernel(rate, offs, q, k, v, qp, kvp):
    for h in range(q.shape[0] // HD):
        rows = slice(h * HD, (h + 1) * HD)
        sel = sel_matrix(offs[h], rate, q.shape[1], qp.shape[1])
        got = dot(jnp.concatenate([q[rows, :], k[rows, :], v[rows, :]], axis=0), sel, 1, 0)
        got = got.astype(BF)
        qp[rows, :] = got[:HD]
        for c in range(kvp.shape[0]):
            kvp[c, 0, rows, :] = got[HD : 2 * HD]
            kvp[c, 1, rows, :] = got[2 * HD :]


def stack_rows(count, parts):
    row = lax.broadcasted_iota(jnp.int32, (count, parts[0].shape[1]), 0)
    out = jnp.zeros(row.shape, F32)
    for i, part in enumerate(parts):
        out = jnp.where(row == i, part.astype(F32), out)
    return out.astype(BF)


def fwd_kernel(info, q, k, v, qp, e_out, out, stats, pa, oa_p, lse_p, kt, qa, va):
    tok = k.shape[1]
    qb = out.shape[1]
    step = pl.program_id(1)

    @pl.when(step == 0)
    def _():
        pos = lax.broadcasted_iota(jnp.int32, (HD, tok), 1) + info[1]
        row = lax.broadcasted_iota(jnp.int32, (HD, tok), 0)
        bias = jnp.where(
            row == 0, jnp.where(pos >= info[0], NEGATIVE, 0.0), jnp.where(row == 1, -1.0, 0.0)
        )
        kt[...] = jnp.concatenate([k[...], bias.astype(BF)], axis=0).T
        one = jnp.where(row == 0, 1.0, 0.0).astype(BF)
        qa[...] = jnp.concatenate([q[...] * jnp.asarray(0.125, BF), one], axis=0)
        first = dot(kt[:256, :], qa[...], 1, 0)
        top = jnp.max(jnp.max(first.reshape(32, 8, tok), axis=0), axis=0, keepdims=True)
        qa[HD:, :] = jnp.where(row == 0, 1.0, jnp.where(row == 1, top, 0.0)).astype(BF)
        row16 = lax.broadcasted_iota(jnp.int32, (16, tok), 0)
        va[...] = jnp.concatenate([v[...], jnp.where(row16 == 0, 1.0, 0.0).astype(BF)], axis=0)

    base = pl.multiple_of(step * qb, qb)

    def finish(cols, acc):
        rt = 1.0 / acc[HD : HD + 1]
        out[:, cols] = acc[:HD] * rt
        stats[0, :, cols] = jnp.broadcast_to(rt, (8, rt.shape[1]))

    qc = qa[:, pl.ds(base, qb)]
    for i in range(0, tok, CK):
        e_out[0, i : i + CK, :] = jnp.exp(dot(kt[i : i + CK, :], qc, 1, 0)).astype(BF)
    acc = dot(va[...], e_out[0], 1, 0)
    finish(slice(0, qb), acc)
    total = acc[HD : HD + 1]
    unsafe = jnp.max(jnp.where(total < SAFE, 0.0, 1.0)) > 0.0

    @pl.when(step == pl.num_programs(1) - 1)
    def _():
        qs = qp[...] * jnp.asarray(0.125, BF)
        here = lax.broadcasted_iota(jnp.int32, (1, tok), 1)
        s = jnp.where(here + info[1] < info[0], dot(qs, k[...], 0, 0), NEGATIVE)
        p, lse = softmax_rows(s)
        pa[0] = p
        oa_p[0] = dot(p, v[...], 1, 1)
        lse_p[0] = jnp.broadcast_to(lse, lse_p.shape[1:])

    @pl.when(unsafe)
    def _():
        width = 128

        def redo(n, carry):
            c0 = pl.multiple_of(n * width, width)
            cols = pl.ds(c0, width)
            s = dot(kt[...], qa[:, pl.ds(pl.multiple_of(base + c0, width), width)], 1, 0)
            s = s - jnp.max(s, axis=0, keepdims=True)
            e_out[0, :, cols] = jnp.exp(s).astype(BF)
            finish(cols, dot(va[...], e_out[0, :, cols], 1, 0))
            return carry

        lax.fori_loop(0, qb // width, redo, 0)


def softmax_rows(s):
    m = jnp.max(s, axis=1, keepdims=True)
    e = jnp.exp(s - m)
    t = jnp.sum(e, axis=1, keepdims=True)
    return (e * (1.0 / t)).astype(BF), m + jnp.log(t)


def far_parts(kv_own, kv_oth, rows):
    both = [ref.at[c] for ref in (kv_own, kv_oth) for c in range(ref.shape[0])]
    return tuple(jnp.concatenate([ref[n, rows, :] for ref in both], axis=1) for n in range(2))


def mid_kernel(
    rate, info, offs, qp, kv_own, kv_oth, stats, w, oa_p, lse_p, k_in, v_in, pa_in, out_a,
    c0, c1, c2, c3, t0, t1, t2, t3, dob, dkp, dvp, kept, sent, dqp,
    k, v, pa, dkp_buf, dvp_buf, wt, attn, pb, g_buf, oa, cot, t_buf, dob_buf, in_sems, out_sems,
):
    part = c0.shape[0]
    count = cot.shape[0] // part
    heads = pa.shape[0]
    tok = attn.shape[1]
    picks = qp.shape[1]
    chips = kv_own.shape[0]
    width = heads * HD
    length, start, core = info[0], info[1], info[3]
    oa_copy = pltpu.make_async_copy(out_a, oa, in_sems.at[count])
    oa_copy.start()
    copies = []
    for s, block in enumerate((c0, c1, c2, c3)):
        owner = lax.rem(info[2] + (count - s), count)
        there = cot.at[pl.ds(pl.multiple_of(owner * part, part), part), :]
        copies.append(pltpu.make_async_copy(block, there, in_sems.at[s]))
        copies[-1].start()
    for n, (there, here) in enumerate(((k_in, k), (v_in, v), (pa_in, pa))):
        copies.append(pltpu.make_async_copy(there, here, in_sems.at[count + 1 + n]))
        copies[-1].start()

    here = lax.broadcasted_iota(jnp.int32, (1, tok), 1)
    keep = jnp.where(here + start < length, 1.0, 0.0)
    num = lax.broadcasted_iota(jnp.int32, (1, 2 * chips * picks), 1)
    chunk = num // picks
    rank = 2 * (chunk % chips) + jnp.where(chunk < chips, core, 1 - core)
    far_pos = (rank * picks + num % picks) * rate
    pick_pos = lax.broadcasted_iota(jnp.int32, (picks, 1), 0) * rate + start
    wt[...] = w[...].T
    kept_parts = []
    mixed_parts = []
    for h in range(heads):
        rows = slice(h * HD, (h + 1) * HD)
        off = offs[h]
        kf, vf = far_parts(kv_own, kv_oth, rows)
        qs = qp[rows, :] * jnp.asarray(0.125, BF)
        p_b, lse_b = softmax_rows(
            jnp.where(far_pos + off < length, dot(qs, kf, 0, 0), NEGATIVE)
        )
        pb[h] = p_b
        o_b = dot(p_b, vf, 1, 1)
        o_a, lse_a = oa_p[h], lse_p[h, :, :1]
        gap = lse_a - lse_b
        near = 1.0 / (1.0 + jnp.exp(-gap))
        far = 1.0 / (1.0 + jnp.exp(gap))
        kept_parts.append((o_a, o_b, near, far))
        live = jnp.where(pick_pos + off < length, 1.0, 0.0)
        mixed_parts.append(((near * o_a + far * o_b) * live).astype(BF))
    oa_copy.wait()
    for h in range(heads):
        rows = slice(h * HD, (h + 1) * HD)
        spread = dot(mixed_parts[h], place_matrix(offs[h], rate, 0, picks, tok), 0, 0)
        attn[rows, :] = jnp.where(
            (here % rate) == offs[h], spread, oa[rows, :] * keep
        ).astype(BF)
    sends = []
    for s, term in enumerate((t0, t1, t2, t3)):
        owner = lax.rem(info[2] + s, count)
        out_rows = pl.ds(pl.multiple_of(owner * part, part), part)
        t_buf[s] = dot(wt[out_rows, :], attn[...], 1, 0).astype(BF)
        sends.append(pltpu.make_async_copy(t_buf.at[s], term, out_sems.at[s]))
        sends[-1].start()

    for copy in copies[:count]:
        copy.wait()
    for h in range(heads):
        rows = slice(h * HD, (h + 1) * HD)
        g_all = dot(w[rows, :], cot[...], 1, 0).astype(BF).astype(F32) * keep
        g_buf[rows, :] = g_all.astype(BF)
        g = jnp.where((here % rate) == offs[h], 0.0, g_all)
        rt = stats[h, 0:1, :]
        delta = jnp.sum(g * oa[rows, :], axis=0, keepdims=True)
        c_hi, c_lo = split2(-delta * rt)
        dob_buf[h] = jnp.concatenate(
            [(g * rt).astype(BF), stack_rows(HD, [c_hi, c_lo])], axis=0
        )
    sends.append(pltpu.make_async_copy(dob_buf, dob, out_sems.at[count]))
    sends[-1].start()

    for copy in copies[count:]:
        copy.wait()
    for h in range(heads):
        rows = slice(h * HD, (h + 1) * HD)
        g = dot(sel_matrix(offs[h], rate, tok, picks), g_buf[rows, :], 0, 1)
        o_a, o_b, near, far = kept_parts[h]
        dlse = near * far * jnp.sum(g * (o_a - o_b), axis=1, keepdims=True)
        kf, vf = far_parts(kv_own, kv_oth, rows)
        q = qp[rows, :]

        def back(k_all, v_all, p, do, out, dl):
            delta = jnp.sum(do.astype(F32) * out, axis=1, keepdims=True)
            dp = dot(do, v_all, 1, 0) + (dl - delta)
            ds = (p.astype(F32) * dp * 0.125).astype(BF)
            return dot(ds, k_all, 1, 1), dot(q, ds, 1, 0), dot(do, p, 0, 0)

        dq_a, dk_a, dv_a = back(k[rows, :], v[rows, :], pa[h], (near * g).astype(BF), o_a, dlse)
        dq_b, dk_b, dv_b = back(kf, vf, pb[h], (far * g).astype(BF), o_b, -dlse)
        dqp[h] = (dq_a + dq_b).astype(BF)
        dkp_buf[rows, :] = dk_a.astype(BF)
        dvp_buf[rows, :] = dv_a.astype(BF)
        for n, grad in enumerate((dk_b.astype(BF), dv_b.astype(BF))):
            first = n * width + h * HD
            for i, ref in enumerate((kept, sent)):
                for c in range(chips):
                    cols = slice((i * chips + c) * picks, (i * chips + c + 1) * picks)
                    ref[c, first : first + HD, :] = grad[:, cols]
    for n, (buf, out) in enumerate(((dkp_buf, dkp), (dvp_buf, dvp))):
        sends.append(pltpu.make_async_copy(buf, out, out_sems.at[count + 1 + n]))
        sends[-1].start()
    grad = dot(attn[...], cot[...], 1, 1)
    size = grad.shape[0] // chips
    half = grad.shape[1] // 2
    blank = jnp.zeros((32 - size, picks), F32)
    for side in range(2):

        @pl.when(core == side)
        def _():
            for ref, parity in ((kept, side), (sent, 1 - side)):
                for c in range(chips):
                    for n in range(half // picks):
                        left = parity * half + n * picks
                        piece = grad[c * size : (c + 1) * size, left : left + picks]
                        first = 2 * width + 32 * n
                        ref[c, first : first + 32, :] = jnp.concatenate(
                            [piece, blank], axis=0
                        ).astype(BF)
    for send in sends:
        send.wait()


def bwd_step(rate, off, e, dob, q, k, v, dqp, dkp, dvp, dq, dk, dv, vt):
    tok = k.shape[1]
    qb = q.shape[1]
    step = pl.program_id(1)

    @pl.when(step == 0)
    def _():
        row = lax.broadcasted_iota(jnp.int32, (HD, tok), 0)
        ones = jnp.where(row < 2, 1.0, 0.0).astype(BF)
        vt[...] = jnp.concatenate([v[...], ones], axis=0).T
        dk[...] = dkp[...].astype(F32) * 8.0
        dv[...] = dvp[...].astype(F32)

    do = dob[0, :HD, :]
    acc = None
    for i in range(0, tok, CK):
        dp = dot(vt[i : i + CK, :], dob[0], 1, 0)
        ei = e[0, i : i + CK, :]
        ds = (ei.astype(F32) * dp).astype(BF)
        part = dot(k[:, i : i + CK], ds, 1, 0)
        acc = part if acc is None else acc + part
        dk[:, i : i + CK] += dot(q[...], ds, 1, 1)
        dv[:, i : i + CK] += dot(do, ei, 1, 1)
    place = place_matrix(off, rate, step * qb, dqp.shape[1], qb)
    dq[...] = (acc * 0.125 + dot(dqp[0], place, 0, 0)).astype(BF)


def bwd_kernel(rate, offs, e, dob, q, k, v, dqp, dkp, dvp, dq, dk, dv, vt):
    off = offs[pl.program_id(0)]
    bwd_step(rate, off, e, dob, q, k, v, dqp, dkp, dvp, dq, dk, dv, vt)


def far_sum(rate, off, far_k, far_v, tok):
    sums = []
    for parts in (far_k, far_v):
        total = parts[0].astype(F32)
        for r in range(1, parts.shape[0]):
            total = total + parts[r].astype(F32)
        sums.append(total.astype(BF))
    place = place_matrix(off, rate, 0, far_k.shape[2], tok)
    return dot(jnp.concatenate(sums, axis=0), place, 1, 0)


def last_kernel(
    rate, last, offs, e, dob, q, k, v, dqp, dkp, dvp, far_k, far_v,
    dk_old, dv_old, old_k, old_v, t0, t1, t2, t3, dq_old,
    dq, kg, vg, mixed, dk, dv, k_buf, v_buf, vt, sems, t_buf, t_sems,
):
    tok = k.shape[1]
    step = pl.program_id(1)
    size = mixed.shape[0]
    slab = pl.ds(pl.multiple_of(step * size, size), size)
    loads = [
        pltpu.make_async_copy(t.at[slab, :], t_buf.at[n], t_sems.at[n])
        for n, t in enumerate((t0, t1, t2, t3))
    ]
    for load in loads:
        load.start()
    bwd_step(rate, offs[last], e, dob, q, k, v, dqp, dkp, dvp, dq, dk, dv, vt)

    def store(slot, head, near_k, near_v, spread):
        k_buf[slot] = (near_k * 0.125 + spread[:HD]).astype(BF)
        v_buf[slot] = (near_v + spread[HD:]).astype(BF)
        rows = pl.ds(pl.multiple_of(head * HD, HD), HD)
        for n, (buf, out) in enumerate(((k_buf, kg), (v_buf, vg))):
            pltpu.make_async_copy(buf.at[slot], out.at[rows, :], sems.at[slot, n]).start()

    def wait(slot):
        for n, (buf, out) in enumerate(((k_buf, kg), (v_buf, vg))):
            pltpu.make_async_copy(buf.at[slot], out.at[:HD, :], sems.at[slot, n]).wait()

    store(step, step, dk_old[...], dv_old[...], far_sum(rate, offs[step], old_k, old_v, tok))
    for load in loads:
        load.wait()
    total = t_buf[0].astype(F32)
    for n in range(1, len(loads)):
        total = total + t_buf[n].astype(F32)
    mixed[...] = total.astype(BF)

    @pl.when(step == last - 1)
    def _():
        store(last, last, dk[...], dv[...], far_sum(rate, offs[last], far_k, far_v, tok))
        for slot in range(last + 1):
            wait(slot)


SDS = jax.ShapeDtypeStruct


def pick(rate, offs, q, k, v, picks, copies):
    rows = q.shape[0]
    return call(
        lambda *r: pick_kernel(rate, *r), "pick", (), [SMEM] + [WHOLE] * 3, [WHOLE] * 2,
        [SDS((rows, picks), BF), SDS((copies, 2, rows, picks), BF)], us=2,
    )(offs, q, k, v)


def forward(info, q, k, v, qp):
    rows, tok = q.shape
    heads = rows // HD
    picks = qp.shape[1]
    qb = min(QB, tok)
    by_q = pl.BlockSpec((HD, qb), lambda h, j: (h, j))
    whole = pl.BlockSpec((HD, tok), lambda h, j: (h, 0))
    by_h = lambda n: pl.BlockSpec((1, picks, n), lambda h, j: (h, 0, 0))
    return call(
        fwd_kernel, "fwd", (heads, tok // qb),
        [SMEM, whole, whole, whole, pl.BlockSpec((HD, picks), lambda h, j: (h, 0))],
        [
            pl.BlockSpec((1, tok, qb), lambda h, j: (h, 0, j)),
            by_q,
            pl.BlockSpec((1, 8, qb), lambda h, j: (h, 0, j)),
            by_h(tok), by_h(HD), by_h(HD),
        ],
        [
            SDS((heads, tok, tok), BF), SDS((rows, tok), F32), SDS((heads, 8, tok), F32),
            SDS((heads, picks, tok), BF), SDS((heads, picks, HD), F32),
            SDS((heads, picks, HD), F32),
        ],
        scratch=[
            pltpu.VMEM((tok, 2 * HD), BF), pltpu.VMEM((2 * HD, tok), BF),
            pltpu.VMEM((HD + 16, tok), BF),
        ],
        us=18,
    )(info, q, k, v, qp)


def middle(rate, info, offs, qp, kv_own, kv_oth, k, v, stats, w, near, out_a, blocks):
    rows, tok = k.shape
    heads = rows // HD
    picks = qp.shape[1]
    count = len(blocks)
    chips = kv_own.shape[0]
    far = 2 * chips * picks
    anywhere = pl.BlockSpec(memory_space=pl.ANY)
    half = SDS((chips, 2 * rows + 16 * (count * rows // picks), picks), BF)
    dob = (heads, 2 * HD, tok)
    return call(
        lambda *r: mid_kernel(rate, *r), "mid", (),
        [SMEM, SMEM] + [WHOLE] * 7 + [anywhere] * 8,
        [anywhere] * 7 + [WHOLE] * 3,
        [SDS((rows, tok), BF)] * count
        + [
            SDS(dob, BF), SDS((rows, tok), BF), SDS((rows, tok), BF), half, half,
            SDS((heads, picks, HD), BF),
        ],
        scratch=[
            pltpu.VMEM((rows, tok), BF), pltpu.VMEM((rows, tok), BF),
            pltpu.VMEM((heads, picks, tok), BF), pltpu.VMEM((rows, tok), BF),
            pltpu.VMEM((rows, tok), BF), pltpu.VMEM((count * rows, rows), BF),
            pltpu.VMEM((rows, tok), BF), pltpu.VMEM((heads, picks, far), BF),
            pltpu.VMEM((rows, tok), BF), pltpu.VMEM((rows, tok), F32),
            pltpu.VMEM((count * rows, tok), BF), pltpu.VMEM((count, rows, tok), BF),
            pltpu.VMEM(dob, BF), pltpu.SemaphoreType.DMA((count + 4,)),
            pltpu.SemaphoreType.DMA((count + 3,)),
        ],
        us=16,
    )(info, offs, qp, kv_own, kv_oth, stats, w, *near[1:], k, v, near[0], out_a, *blocks)


def hold_all(arrays, after):
    anywhere = pl.BlockSpec(memory_space=pl.ANY)
    count = len(arrays)
    return pl.pallas_call(
        lambda *refs: None, name="hold", in_specs=[anywhere] * (count + 1),
        out_specs=[anywhere] * count, out_shape=[SDS(x.shape, x.dtype) for x in arrays],
        input_output_aliases={i: i for i in range(count)},
    )(*arrays, after)


def hold(x, after):
    return hold_all([x], after)[0]


def total_kernel(parts, after, out):
    total = parts[0].astype(F32)
    for r in range(1, parts.shape[0]):
        total = total + parts[r].astype(F32)
    cols = total.shape[1]
    mine = jnp.concatenate(
        [total[r : r + out.shape[1]] for r in range(0, total.shape[0], 32)], axis=1
    )
    for r in range(out.shape[0]):
        out[r] = mine


def total(parts, first, size, copies, after):
    count, rows, cols = parts.shape
    rows -= first
    shape = (copies, size, rows // 32 * cols)
    return call(
        total_kernel, "total", (1,),
        [
            pl.BlockSpec((count, rows, cols), lambda i: (0, first // rows, 0)),
            pl.BlockSpec(memory_space=pl.ANY),
        ],
        pl.BlockSpec(shape, lambda i: (0, 0, 0)),
        SDS(shape, F32), us=1, mib=8,
    )(parts, after)


def spread_kernel(scale, parts, out):
    mine = parts[0]
    for r in range(1, parts.shape[0]):
        mine = mine + parts[r]
    mine = mine * scale
    for r in range(out.shape[0]):
        out[r] = mine


def spread_sum(scale, parts, copies):
    return call(
        lambda *r: spread_kernel(scale, *r), "spread", (), [WHOLE], WHOLE,
        SDS((copies,) + parts.shape[1:], F32), us=1, mib=8,
    )(parts)


def backward_specs(first, rows, tok, picks):
    qb = min(QB, tok)
    by_q = pl.BlockSpec((HD, qb), lambda h, j: (first + h, j))
    whole = pl.BlockSpec((HD, tok), lambda h, j: (first + h, 0))
    ins = [
        SMEM,
        pl.BlockSpec((1, tok, qb), lambda h, j: (first + h, 0, j)),
        pl.BlockSpec((1, 2 * HD, qb), lambda h, j: (first + h, 0, j)),
        by_q, whole, whole, pl.BlockSpec((1, picks, HD), lambda h, j: (first + h, 0, 0)),
        whole, whole,
    ]
    return qb, by_q, whole, ins


def backward(heads, rate, offs, e, dob, q, k, v, dqp, dkp, dvp, after):
    rows, tok = q.shape
    qb, by_q, whole, ins = backward_specs(0, rows, tok, dqp.shape[1])
    spare = [pl.BlockSpec(memory_space=pl.ANY)] * len(after)

    def kernel(*refs):
        bwd_kernel(rate, *refs[:9], *refs[9 + len(after) :])

    return call(
        kernel, "bwd", (heads, tok // qb), ins + spare, [by_q, whole, whole],
        [SDS((rows, tok), BF)] + [SDS((heads * HD, tok), F32)] * 2,
        scratch=[pltpu.VMEM((tok, 2 * HD), BF)],
        us=11 * heads,
    )(offs, e, dob, q, k, v, dqp, dkp, dvp, *after)


def backward_last(rate, offs, e, dob, q, k, v, dqp, dkp, dvp, far, dq_old, dk_old, dv_old, terms):
    rows, tok = q.shape
    heads = rows // HD
    last = heads - 1
    chips, _, picks = far.shape
    qb, by_q, whole, ins = backward_specs(last, rows, tok, picks)
    assert tok // qb == last
    anywhere = pl.BlockSpec(memory_space=pl.ANY)
    of = lambda at: pl.BlockSpec((chips, HD, picks), lambda h, j: (0, at(j), 0))
    old = pl.BlockSpec((HD, tok), lambda h, j: (j, 0))
    slab = pl.BlockSpec((rows // last, tok), lambda h, j: (j, 0))
    ins = ins + [of(lambda j: last), of(lambda j: heads + last), old, old]
    ins = ins + [of(lambda j: j), of(lambda j: heads + j)] + [anywhere] * len(terms) + [anywhere]
    buf = pltpu.VMEM((heads, HD, tok), BF)
    return pl.pallas_call(
        lambda *r: last_kernel(rate, last, *r),
        name="last",
        grid=(1, tok // qb),
        in_specs=ins,
        out_specs=[by_q, anywhere, anywhere, slab],
        out_shape=[SDS((rows, tok), BF)] * 4,
        scratch_shapes=[
            pltpu.VMEM((HD, tok), F32), pltpu.VMEM((HD, tok), F32), buf, buf,
            pltpu.VMEM((tok, 2 * HD), BF), pltpu.SemaphoreType.DMA((heads, 2)),
            pltpu.VMEM((len(terms), rows // last, tok), BF),
            pltpu.SemaphoreType.DMA((len(terms),)),
        ],
        input_output_aliases={len(ins) - 1: 0},
        compiler_params=pltpu.CompilerParams(vmem_limit_bytes=VMEM_BYTES),
        cost_estimate=work(13),
    )(offs, e, dob, q, k, v, dqp, dkp, dvp, far, far, dk_old, dv_old, far, far, *terms, dq_old)


def shift(x, axis, by):
    count = lax.axis_size(axis)
    return lax.ppermute(x, axis, [(i, (i + by) % count) for i in range(count)])


def shards(queries, keys, values, cotangent, w_out, lengths, offsets):
    rows, tok = queries.shape[1:]
    seq_count = lax.axis_size("seq")
    rate = tok * seq_count // SEL
    picks = tok // rate
    place = lax.axis_index("seq").astype(jnp.int32)
    info = jnp.stack(
        [
            lengths[0], place * tok, lax.axis_index("head").astype(jnp.int32), place % 2,
            place // 2,
        ]
    )
    q, k, v = queries[0], keys[0], values[0]
    groups = [list(range(c, seq_count, 2)) for c in range(2)]
    chips = seq_count // 2
    swap = [(i, i ^ 1) for i in range(seq_count)]
    qp, kvp = pick(rate, offsets, q, k, v, picks, chips)
    kv_own = lax.all_to_all(kvp, "seq", 0, 0, axis_index_groups=groups)
    own = cotangent[0]
    blocks = [own] + [shift(own, "head", s) for s in (1, 2, 3)]
    e, out_a, stats, *near = forward(info, q, k, v, qp)
    kv_own = hold(kv_own, stats)
    kv_oth = lax.ppermute(kv_own, "seq", swap)
    *terms, dob, dkp, dvp, kept, sent, dqp = middle(
        rate, info, offsets, qp, kv_own, kv_oth, k, v, stats, w_out, near, out_a, blocks
    )
    got = lax.ppermute(sent, "seq", swap)
    pair = kept + got
    far = lax.all_to_all(pair, "seq", 0, 0, axis_index_groups=groups)
    later = hold_all(terms[1:], pair)
    terms = terms[:1] + [shift(t, "head", s + 1) for s, t in enumerate(later)]
    dq, dk, dv = backward(2, rate, offsets, e, dob, q, k, v, dqp, dkp, dvp, (pair,))
    grad_scale = 1.0 / math.sqrt(tok * seq_count * lax.axis_size("dp"))
    mine = total(far, 2 * rows, rows // chips, lax.axis_size("dp"), dk)
    mine = lax.all_to_all(mine, "dp", 0, 0)
    spread = lax.all_to_all(spread_sum(grad_scale, mine, seq_count), "seq", 0, 0)
    spread = spread.reshape((chips, 2) + spread.shape[1:])
    weight_grad = spread.transpose(0, 2, 1, 3).reshape(w_out.shape)
    dq, kg, vg, mixed = backward_last(
        rate, offsets, e, dob, q, k, v, dqp, dkp, dvp, far, dq, dk, dv, terms
    )
    return (mixed[None], dq[None], kg[None], vg[None], weight_grad)


def solution(mesh):
    full = P("dp", "head", "seq")
    return jax.shard_map(
        shards,
        mesh=mesh,
        in_specs=(full, full, full, full, P("head", None), P("dp"), P("head")),
        out_specs=(full, full, full, full, P("head", None)),
        check_vma=False,
    )
```

```python
import math

import jax
import jax.numpy as jnp
from jax import lax
from jax.experimental import pallas as pl
from jax.experimental.pallas import tpu as pltpu
from jax.sharding import PartitionSpec as P

SEL = 2048
HD = 64
NEGATIVE = -1e30
BF = jnp.bfloat16
F32 = jnp.float32
QB = 1024
CK = 512
SAFE = 2.0**40
VMEM_BYTES = 60 * 2**20


def dot(a, b, ca, cb):
    return lax.dot_general(a, b, (((ca,), (cb,)), ((), ())), preferred_element_type=F32)


def split2(x):
    hi = x.astype(BF)
    return hi, (x - hi.astype(F32)).astype(BF)


def split3(x):
    hi = x.astype(BF)
    rest = x - hi.astype(F32)
    mid = rest.astype(BF)
    return hi, mid, (rest - mid.astype(F32)).astype(BF)


def call(kern, name, grid, in_specs, out_specs, out_shape, scratch=(), us=1, mib=60):
    return pl.pallas_call(
        kern,
        name=name,
        grid=grid,
        in_specs=in_specs,
        out_specs=out_specs,
        out_shape=out_shape,
        scratch_shapes=list(scratch),
        compiler_params=pltpu.CompilerParams(vmem_limit_bytes=mib * 2**20),
        cost_estimate=work(us),
    )


def work(us):
    return pl.CostEstimate(flops=int(us * 1.15e9), bytes_accessed=0, transcendentals=0)


SMEM = pl.BlockSpec(memory_space=pltpu.SMEM)
WHOLE = pl.BlockSpec(memory_space=pltpu.VMEM)


def sel_matrix(off, rate, rows, cols):
    pos = lax.broadcasted_iota(jnp.int32, (rows, cols), 0)
    num = lax.broadcasted_iota(jnp.int32, (rows, cols), 1)
    return jnp.where(pos == num * rate + off, 1.0, 0.0).astype(BF)


def place_matrix(off, rate, start, rows, cols):
    num = lax.broadcasted_iota(jnp.int32, (rows, cols), 0)
    pos = lax.broadcasted_iota(jnp.int32, (rows, cols), 1) + start
    return jnp.where(pos == num * rate + off, 1.0, 0.0).astype(BF)


def pick_kernel(rate, offs, q, k, v, qp, kvp):
    for h in range(q.shape[0] // HD):
        rows = slice(h * HD, (h + 1) * HD)
        sel = sel_matrix(offs[h], rate, q.shape[1], qp.shape[1])
        got = dot(jnp.concatenate([q[rows, :], k[rows, :], v[rows, :]], axis=0), sel, 1, 0)
        got = got.astype(BF)
        qp[rows, :] = got[:HD]
        for c in range(kvp.shape[0]):
            kvp[c, 0, rows, :] = got[HD : 2 * HD]
            kvp[c, 1, rows, :] = got[2 * HD :]


def stack_rows(count, parts):
    row = lax.broadcasted_iota(jnp.int32, (count, parts[0].shape[1]), 0)
    out = jnp.zeros(row.shape, F32)
    for i, part in enumerate(parts):
        out = jnp.where(row == i, part.astype(F32), out)
    return out.astype(BF)


def fwd_kernel(info, q, k, v, qp, e_out, out, stats, pa, oa_p, lse_p, kt, qa, va):
    tok = k.shape[1]
    qb = out.shape[1]
    step = pl.program_id(1)

    @pl.when(step == 0)
    def _():
        pos = lax.broadcasted_iota(jnp.int32, (HD, tok), 1) + info[1]
        row = lax.broadcasted_iota(jnp.int32, (HD, tok), 0)
        bias = jnp.where(
            row == 0, jnp.where(pos >= info[0], NEGATIVE, 0.0), jnp.where(row == 1, -1.0, 0.0)
        )
        kt[...] = jnp.concatenate([k[...], bias.astype(BF)], axis=0).T
        one = jnp.where(row == 0, 1.0, 0.0).astype(BF)
        qa[...] = jnp.concatenate([q[...] * jnp.asarray(0.125, BF), one], axis=0)
        first = dot(kt[:256, :], qa[...], 1, 0)
        top = jnp.max(jnp.max(first.reshape(32, 8, tok), axis=0), axis=0, keepdims=True)
        qa[HD:, :] = jnp.where(row == 0, 1.0, jnp.where(row == 1, top, 0.0)).astype(BF)
        row16 = lax.broadcasted_iota(jnp.int32, (16, tok), 0)
        va[...] = jnp.concatenate([v[...], jnp.where(row16 == 0, 1.0, 0.0).astype(BF)], axis=0)

    base = pl.multiple_of(step * qb, qb)

    def finish(cols, acc):
        rt = 1.0 / acc[HD : HD + 1]
        out[:, cols] = acc[:HD] * rt
        stats[0, :, cols] = jnp.broadcast_to(rt, (8, rt.shape[1]))

    qc = qa[:, pl.ds(base, qb)]
    for i in range(0, tok, CK):
        e_out[0, i : i + CK, :] = jnp.exp(dot(kt[i : i + CK, :], qc, 1, 0)).astype(BF)
    acc = dot(va[...], e_out[0], 1, 0)
    finish(slice(0, qb), acc)
    total = acc[HD : HD + 1]
    unsafe = jnp.max(jnp.where(total < SAFE, 0.0, 1.0)) > 0.0

    @pl.when(step == pl.num_programs(1) - 1)
    def _():
        qs = qp[...] * jnp.asarray(0.125, BF)
        here = lax.broadcasted_iota(jnp.int32, (1, tok), 1)
        s = jnp.where(here + info[1] < info[0], dot(qs, k[...], 0, 0), NEGATIVE)
        p, lse = softmax_rows(s)
        pa[0] = p
        oa_p[0] = dot(p, v[...], 1, 1)
        lse_p[0] = jnp.broadcast_to(lse, lse_p.shape[1:])

    @pl.when(unsafe)
    def _():
        width = 128

        def redo(n, carry):
            c0 = pl.multiple_of(n * width, width)
            cols = pl.ds(c0, width)
            s = dot(kt[...], qa[:, pl.ds(pl.multiple_of(base + c0, width), width)], 1, 0)
            s = s - jnp.max(s, axis=0, keepdims=True)
            e_out[0, :, cols] = jnp.exp(s).astype(BF)
            finish(cols, dot(va[...], e_out[0, :, cols], 1, 0))
            return carry

        lax.fori_loop(0, qb // width, redo, 0)


def softmax_rows(s):
    m = jnp.max(s, axis=1, keepdims=True)
    e = jnp.exp(s - m)
    t = jnp.sum(e, axis=1, keepdims=True)
    return (e * (1.0 / t)).astype(BF), m + jnp.log(t)


def far_parts(kv_own, kv_oth, rows):
    both = [ref.at[c] for ref in (kv_own, kv_oth) for c in range(ref.shape[0])]
    return tuple(jnp.concatenate([ref[n, rows, :] for ref in both], axis=1) for n in range(2))


def mid_kernel(
    rate, info, offs, qp, kv_own, kv_oth, stats, w, oa_p, lse_p, k_in, v_in, pa_in, out_a,
    c0, c1, c2, c3, t0, t1, t2, t3, dob, dkp, dvp, kept, sent, dqp,
    k, v, pa, dkp_buf, dvp_buf, wt, attn, pb, g_buf, oa, cot, t_buf, dob_buf, in_sems, out_sems,
):
    part = c0.shape[0]
    count = cot.shape[0] // part
    heads = pa.shape[0]
    tok = attn.shape[1]
    picks = qp.shape[1]
    chips = kv_own.shape[0]
    width = heads * HD
    length, start, core = info[0], info[1], info[3]
    oa_copy = pltpu.make_async_copy(out_a, oa, in_sems.at[count])
    oa_copy.start()
    copies = []
    for s, block in enumerate((c0, c1, c2, c3)):
        owner = lax.rem(info[2] + (count - s), count)
        there = cot.at[pl.ds(pl.multiple_of(owner * part, part), part), :]
        copies.append(pltpu.make_async_copy(block, there, in_sems.at[s]))
        copies[-1].start()
    for n, (there, here) in enumerate(((k_in, k), (v_in, v), (pa_in, pa))):
        copies.append(pltpu.make_async_copy(there, here, in_sems.at[count + 1 + n]))
        copies[-1].start()

    here = lax.broadcasted_iota(jnp.int32, (1, tok), 1)
    keep = jnp.where(here + start < length, 1.0, 0.0)
    num = lax.broadcasted_iota(jnp.int32, (1, 2 * chips * picks), 1)
    chunk = num // picks
    rank = 2 * (chunk % chips) + jnp.where(chunk < chips, core, 1 - core)
    far_pos = (rank * picks + num % picks) * rate
    pick_pos = lax.broadcasted_iota(jnp.int32, (picks, 1), 0) * rate + start
    wt[...] = w[...].T
    kept_parts = []
    mixed_parts = []
    for h in range(heads):
        rows = slice(h * HD, (h + 1) * HD)
        off = offs[h]
        kf, vf = far_parts(kv_own, kv_oth, rows)
        qs = qp[rows, :] * jnp.asarray(0.125, BF)
        p_b, lse_b = softmax_rows(
            jnp.where(far_pos + off < length, dot(qs, kf, 0, 0), NEGATIVE)
        )
        pb[h] = p_b
        o_b = dot(p_b, vf, 1, 1)
        o_a, lse_a = oa_p[h], lse_p[h, :, :1]
        gap = lse_a - lse_b
        near = 1.0 / (1.0 + jnp.exp(-gap))
        far = 1.0 / (1.0 + jnp.exp(gap))
        kept_parts.append((o_a, o_b, near, far))
        live = jnp.where(pick_pos + off < length, 1.0, 0.0)
        mixed_parts.append(((near * o_a + far * o_b) * live).astype(BF))
    oa_copy.wait()
    for h in range(heads):
        rows = slice(h * HD, (h + 1) * HD)
        spread = dot(mixed_parts[h], place_matrix(offs[h], rate, 0, picks, tok), 0, 0)
        attn[rows, :] = jnp.where(
            (here % rate) == offs[h], spread, oa[rows, :] * keep
        ).astype(BF)
    sends = []
    for s, term in enumerate((t0, t1, t2, t3)):
        owner = lax.rem(info[2] + s, count)
        out_rows = pl.ds(pl.multiple_of(owner * part, part), part)
        t_buf[s] = dot(wt[out_rows, :], attn[...], 1, 0).astype(BF)
        sends.append(pltpu.make_async_copy(t_buf.at[s], term, out_sems.at[s]))
        sends[-1].start()

    for copy in copies[:count]:
        copy.wait()
    for h in range(heads):
        rows = slice(h * HD, (h + 1) * HD)
        g_all = dot(w[rows, :], cot[...], 1, 0).astype(BF).astype(F32) * keep
        g_buf[rows, :] = g_all.astype(BF)
        g = jnp.where((here % rate) == offs[h], 0.0, g_all)
        rt = stats[h, 0:1, :]
        delta = jnp.sum(g * oa[rows, :], axis=0, keepdims=True)
        c_hi, c_lo = split2(-delta * rt)
        dob_buf[h] = jnp.concatenate(
            [(g * rt).astype(BF), stack_rows(HD, [c_hi, c_lo])], axis=0
        )
    sends.append(pltpu.make_async_copy(dob_buf, dob, out_sems.at[count]))
    sends[-1].start()

    for copy in copies[count:]:
        copy.wait()
    for h in range(heads):
        rows = slice(h * HD, (h + 1) * HD)
        g = dot(sel_matrix(offs[h], rate, tok, picks), g_buf[rows, :], 0, 1)
        o_a, o_b, near, far = kept_parts[h]
        dlse = near * far * jnp.sum(g * (o_a - o_b), axis=1, keepdims=True)
        kf, vf = far_parts(kv_own, kv_oth, rows)
        q = qp[rows, :]

        def back(k_all, v_all, p, do, out, dl):
            delta = jnp.sum(do.astype(F32) * out, axis=1, keepdims=True)
            dp = dot(do, v_all, 1, 0) + (dl - delta)
            ds = (p.astype(F32) * dp * 0.125).astype(BF)
            return dot(ds, k_all, 1, 1), dot(q, ds, 1, 0), dot(do, p, 0, 0)

        dq_a, dk_a, dv_a = back(k[rows, :], v[rows, :], pa[h], (near * g).astype(BF), o_a, dlse)
        dq_b, dk_b, dv_b = back(kf, vf, pb[h], (far * g).astype(BF), o_b, -dlse)
        dqp[h] = (dq_a + dq_b).astype(BF)
        dkp_buf[rows, :] = dk_a.astype(BF)
        dvp_buf[rows, :] = dv_a.astype(BF)
        for n, grad in enumerate((dk_b.astype(BF), dv_b.astype(BF))):
            first = n * width + h * HD
            for i, ref in enumerate((kept, sent)):
                for c in range(chips):
                    cols = slice((i * chips + c) * picks, (i * chips + c + 1) * picks)
                    ref[c, first : first + HD, :] = grad[:, cols]
    for n, (buf, out) in enumerate(((dkp_buf, dkp), (dvp_buf, dvp))):
        sends.append(pltpu.make_async_copy(buf, out, out_sems.at[count + 1 + n]))
        sends[-1].start()
    grad = dot(attn[...], cot[...], 1, 1)
    size = grad.shape[0] // chips
    half = grad.shape[1] // 2
    blank = jnp.zeros((32 - size, picks), F32)
    for side in range(2):

        @pl.when(core == side)
        def _():
            for ref, parity in ((kept, side), (sent, 1 - side)):
                for c in range(chips):
                    for n in range(half // picks):
                        left = parity * half + n * picks
                        piece = grad[c * size : (c + 1) * size, left : left + picks]
                        first = 2 * width + 32 * n
                        ref[c, first : first + 32, :] = jnp.concatenate(
                            [piece, blank], axis=0
                        ).astype(BF)
    for send in sends:
        send.wait()


def bwd_step(rate, off, e, dob, q, k, v, dqp, dkp, dvp, dq, dk, dv, vt):
    tok = k.shape[1]
    qb = q.shape[1]
    step = pl.program_id(1)

    @pl.when(step == 0)
    def _():
        row = lax.broadcasted_iota(jnp.int32, (HD, tok), 0)
        ones = jnp.where(row < 2, 1.0, 0.0).astype(BF)
        vt[...] = jnp.concatenate([v[...], ones], axis=0).T
        dk[...] = dkp[...].astype(F32) * 8.0
        dv[...] = dvp[...].astype(F32)

    do = dob[0, :HD, :]
    acc = None
    for i in range(0, tok, CK):
        dp = dot(vt[i : i + CK, :], dob[0], 1, 0)
        ei = e[0, i : i + CK, :]
        ds = (ei.astype(F32) * dp).astype(BF)
        part = dot(k[:, i : i + CK], ds, 1, 0)
        acc = part if acc is None else acc + part
        dk[:, i : i + CK] += dot(q[...], ds, 1, 1)
        dv[:, i : i + CK] += dot(do, ei, 1, 1)
    place = place_matrix(off, rate, step * qb, dqp.shape[1], qb)
    dq[...] = (acc * 0.125 + dot(dqp[0], place, 0, 0)).astype(BF)


def bwd_kernel(rate, offs, e, dob, q, k, v, dqp, dkp, dvp, dq, dk, dv, vt):
    off = offs[pl.program_id(0)]
    bwd_step(rate, off, e, dob, q, k, v, dqp, dkp, dvp, dq, dk, dv, vt)


def far_sum(rate, off, far_k, far_v, tok):
    sums = []
    for parts in (far_k, far_v):
        total = parts[0].astype(F32)
        for r in range(1, parts.shape[0]):
            total = total + parts[r].astype(F32)
        sums.append(total.astype(BF))
    place = place_matrix(off, rate, 0, far_k.shape[2], tok)
    return dot(jnp.concatenate(sums, axis=0), place, 1, 0)


def last_kernel(
    rate, last, offs, e, dob, q, k, v, dqp, dkp, dvp, far_k, far_v,
    dk_old, dv_old, old_k, old_v, t0, t1, t2, t3, dq_old,
    dq, kg, vg, mixed, dk, dv, k_buf, v_buf, vt, sems, t_buf, t_sems,
):
    tok = k.shape[1]
    step = pl.program_id(1)
    size = mixed.shape[0]
    slab = pl.ds(pl.multiple_of(step * size, size), size)
    loads = [
        pltpu.make_async_copy(t.at[slab, :], t_buf.at[n], t_sems.at[n])
        for n, t in enumerate((t0, t1, t2, t3))
    ]
    for load in loads:
        load.start()
    bwd_step(rate, offs[last], e, dob, q, k, v, dqp, dkp, dvp, dq, dk, dv, vt)

    def store(slot, head, near_k, near_v, spread):
        k_buf[slot] = (near_k * 0.125 + spread[:HD]).astype(BF)
        v_buf[slot] = (near_v + spread[HD:]).astype(BF)
        rows = pl.ds(pl.multiple_of(head * HD, HD), HD)
        for n, (buf, out) in enumerate(((k_buf, kg), (v_buf, vg))):
            pltpu.make_async_copy(buf.at[slot], out.at[rows, :], sems.at[slot, n]).start()

    def wait(slot):
        for n, (buf, out) in enumerate(((k_buf, kg), (v_buf, vg))):
            pltpu.make_async_copy(buf.at[slot], out.at[:HD, :], sems.at[slot, n]).wait()

    store(step, step, dk_old[...], dv_old[...], far_sum(rate, offs[step], old_k, old_v, tok))
    for load in loads:
        load.wait()
    total = t_buf[0].astype(F32)
    for n in range(1, len(loads)):
        total = total + t_buf[n].astype(F32)
    mixed[...] = total.astype(BF)

    @pl.when(step == last - 1)
    def _():
        store(last, last, dk[...], dv[...], far_sum(rate, offs[last], far_k, far_v, tok))
        for slot in range(last + 1):
            wait(slot)


SDS = jax.ShapeDtypeStruct


def pick(rate, offs, q, k, v, picks, copies):
    rows = q.shape[0]
    return call(
        lambda *r: pick_kernel(rate, *r), "pick", (), [SMEM] + [WHOLE] * 3, [WHOLE] * 2,
        [SDS((rows, picks), BF), SDS((copies, 2, rows, picks), BF)], us=2,
    )(offs, q, k, v)


def forward(info, q, k, v, qp):
    rows, tok = q.shape
    heads = rows // HD
    picks = qp.shape[1]
    qb = min(QB, tok)
    by_q = pl.BlockSpec((HD, qb), lambda h, j: (h, j))
    whole = pl.BlockSpec((HD, tok), lambda h, j: (h, 0))
    by_h = lambda n: pl.BlockSpec((1, picks, n), lambda h, j: (h, 0, 0))
    return call(
        fwd_kernel, "fwd", (heads, tok // qb),
        [SMEM, whole, whole, whole, pl.BlockSpec((HD, picks), lambda h, j: (h, 0))],
        [
            pl.BlockSpec((1, tok, qb), lambda h, j: (h, 0, j)),
            by_q,
            pl.BlockSpec((1, 8, qb), lambda h, j: (h, 0, j)),
            by_h(tok), by_h(HD), by_h(HD),
        ],
        [
            SDS((heads, tok, tok), BF), SDS((rows, tok), F32), SDS((heads, 8, tok), F32),
            SDS((heads, picks, tok), BF), SDS((heads, picks, HD), F32),
            SDS((heads, picks, HD), F32),
        ],
        scratch=[
            pltpu.VMEM((tok, 2 * HD), BF), pltpu.VMEM((2 * HD, tok), BF),
            pltpu.VMEM((HD + 16, tok), BF),
        ],
        us=18,
    )(info, q, k, v, qp)


def middle(rate, info, offs, qp, kv_own, kv_oth, k, v, stats, w, near, out_a, blocks):
    rows, tok = k.shape
    heads = rows // HD
    picks = qp.shape[1]
    count = len(blocks)
    chips = kv_own.shape[0]
    far = 2 * chips * picks
    anywhere = pl.BlockSpec(memory_space=pl.ANY)
    half = SDS((chips, 2 * rows + 16 * (count * rows // picks), picks), BF)
    dob = (heads, 2 * HD, tok)
    return call(
        lambda *r: mid_kernel(rate, *r), "mid", (),
        [SMEM, SMEM] + [WHOLE] * 7 + [anywhere] * 8,
        [anywhere] * 7 + [WHOLE] * 3,
        [SDS((rows, tok), BF)] * count
        + [
            SDS(dob, BF), SDS((rows, tok), BF), SDS((rows, tok), BF), half, half,
            SDS((heads, picks, HD), BF),
        ],
        scratch=[
            pltpu.VMEM((rows, tok), BF), pltpu.VMEM((rows, tok), BF),
            pltpu.VMEM((heads, picks, tok), BF), pltpu.VMEM((rows, tok), BF),
            pltpu.VMEM((rows, tok), BF), pltpu.VMEM((count * rows, rows), BF),
            pltpu.VMEM((rows, tok), BF), pltpu.VMEM((heads, picks, far), BF),
            pltpu.VMEM((rows, tok), BF), pltpu.VMEM((rows, tok), F32),
            pltpu.VMEM((count * rows, tok), BF), pltpu.VMEM((count, rows, tok), BF),
            pltpu.VMEM(dob, BF), pltpu.SemaphoreType.DMA((count + 4,)),
            pltpu.SemaphoreType.DMA((count + 3,)),
        ],
        us=16,
    )(info, offs, qp, kv_own, kv_oth, stats, w, *near[1:], k, v, near[0], out_a, *blocks)


def hold_all(arrays, after):
    anywhere = pl.BlockSpec(memory_space=pl.ANY)
    count = len(arrays)
    return pl.pallas_call(
        lambda *refs: None, name="hold", in_specs=[anywhere] * (count + 1),
        out_specs=[anywhere] * count, out_shape=[SDS(x.shape, x.dtype) for x in arrays],
        input_output_aliases={i: i for i in range(count)},
    )(*arrays, after)


def hold(x, after):
    return hold_all([x], after)[0]


def total_kernel(parts, after, out):
    total = parts[0].astype(F32)
    for r in range(1, parts.shape[0]):
        total = total + parts[r].astype(F32)
    cols = total.shape[1]
    mine = jnp.concatenate(
        [total[r : r + out.shape[1]] for r in range(0, total.shape[0], 32)], axis=1
    )
    for r in range(out.shape[0]):
        out[r] = mine


def total(parts, first, size, copies, after):
    count, rows, cols = parts.shape
    rows -= first
    shape = (copies, size, rows // 32 * cols)
    return call(
        total_kernel, "total", (1,),
        [
            pl.BlockSpec((count, rows, cols), lambda i: (0, first // rows, 0)),
            pl.BlockSpec(memory_space=pl.ANY),
        ],
        pl.BlockSpec(shape, lambda i: (0, 0, 0)),
        SDS(shape, F32), us=1, mib=8,
    )(parts, after)


def spread_kernel(scale, parts, out):
    mine = parts[0]
    for r in range(1, parts.shape[0]):
        mine = mine + parts[r]
    mine = mine * scale
    for r in range(out.shape[0]):
        out[r] = mine


def spread_sum(scale, parts, copies):
    return call(
        lambda *r: spread_kernel(scale, *r), "spread", (), [WHOLE], WHOLE,
        SDS((copies,) + parts.shape[1:], F32), us=1, mib=8,
    )(parts)


def backward_specs(first, rows, tok, picks):
    qb = min(QB, tok)
    by_q = pl.BlockSpec((HD, qb), lambda h, j: (first + h, j))
    whole = pl.BlockSpec((HD, tok), lambda h, j: (first + h, 0))
    ins = [
        SMEM,
        pl.BlockSpec((1, tok, qb), lambda h, j: (first + h, 0, j)),
        pl.BlockSpec((1, 2 * HD, qb), lambda h, j: (first + h, 0, j)),
        by_q, whole, whole, pl.BlockSpec((1, picks, HD), lambda h, j: (first + h, 0, 0)),
        whole, whole,
    ]
    return qb, by_q, whole, ins


def backward(heads, rate, offs, e, dob, q, k, v, dqp, dkp, dvp, after):
    rows, tok = q.shape
    qb, by_q, whole, ins = backward_specs(0, rows, tok, dqp.shape[1])
    spare = [pl.BlockSpec(memory_space=pl.ANY)] * len(after)

    def kernel(*refs):
        bwd_kernel(rate, *refs[:9], *refs[9 + len(after) :])

    return call(
        kernel, "bwd", (heads, tok // qb), ins + spare, [by_q, whole, whole],
        [SDS((rows, tok), BF)] + [SDS((heads * HD, tok), F32)] * 2,
        scratch=[pltpu.VMEM((tok, 2 * HD), BF)],
        us=11 * heads,
    )(offs, e, dob, q, k, v, dqp, dkp, dvp, *after)


def backward_last(rate, offs, e, dob, q, k, v, dqp, dkp, dvp, far, dq_old, dk_old, dv_old, terms):
    rows, tok = q.shape
    heads = rows // HD
    last = heads - 1
    chips, _, picks = far.shape
    qb, by_q, whole, ins = backward_specs(last, rows, tok, picks)
    assert tok // qb == last
    anywhere = pl.BlockSpec(memory_space=pl.ANY)
    of = lambda at: pl.BlockSpec((chips, HD, picks), lambda h, j: (0, at(j), 0))
    old = pl.BlockSpec((HD, tok), lambda h, j: (j, 0))
    slab = pl.BlockSpec((rows // last, tok), lambda h, j: (j, 0))
    ins = ins + [of(lambda j: last), of(lambda j: heads + last), old, old]
    ins = ins + [of(lambda j: j), of(lambda j: heads + j)] + [anywhere] * len(terms) + [anywhere]
    buf = pltpu.VMEM((heads, HD, tok), BF)
    return pl.pallas_call(
        lambda *r: last_kernel(rate, last, *r),
        name="last",
        grid=(1, tok // qb),
        in_specs=ins,
        out_specs=[by_q, anywhere, anywhere, slab],
        out_shape=[SDS((rows, tok), BF)] * 4,
        scratch_shapes=[
            pltpu.VMEM((HD, tok), F32), pltpu.VMEM((HD, tok), F32), buf, buf,
            pltpu.VMEM((tok, 2 * HD), BF), pltpu.SemaphoreType.DMA((heads, 2)),
            pltpu.VMEM((len(terms), rows // last, tok), BF),
            pltpu.SemaphoreType.DMA((len(terms),)),
        ],
        input_output_aliases={len(ins) - 1: 0},
        compiler_params=pltpu.CompilerParams(vmem_limit_bytes=VMEM_BYTES),
        cost_estimate=work(13),
    )(offs, e, dob, q, k, v, dqp, dkp, dvp, far, far, dk_old, dv_old, far, far, *terms, dq_old)


def shift(x, axis, by):
    count = lax.axis_size(axis)
    return lax.ppermute(x, axis, [(i, (i + by) % count) for i in range(count)])


def shards(queries, keys, values, cotangent, w_out, lengths, offsets):
    rows, tok = queries.shape[1:]
    seq_count = lax.axis_size("seq")
    rate = tok * seq_count // SEL
    picks = tok // rate
    place = lax.axis_index("seq").astype(jnp.int32)
    info = jnp.stack(
        [
            lengths[0], place * tok, lax.axis_index("head").astype(jnp.int32), place % 2,
            place // 2,
        ]
    )
    q, k, v = queries[0], keys[0], values[0]
    groups = [list(range(c, seq_count, 2)) for c in range(2)]
    chips = seq_count // 2
    swap = [(i, i ^ 1) for i in range(seq_count)]
    qp, kvp = pick(rate, offsets, q, k, v, picks, chips)
    kv_own = lax.all_to_all(kvp, "seq", 0, 0, axis_index_groups=groups)
    own = cotangent[0]
    blocks = [own] + [shift(own, "head", s) for s in (1, 2, 3)]
    e, out_a, stats, *near = forward(info, q, k, v, qp)
    kv_own = hold(kv_own, stats)
    kv_oth = lax.ppermute(kv_own, "seq", swap)
    *terms, dob, dkp, dvp, kept, sent, dqp = middle(
        rate, info, offsets, qp, kv_own, kv_oth, k, v, stats, w_out, near, out_a, blocks
    )
    terms = terms[:1] + [shift(terms[s], "head", s) for s in (1, 2, 3)]
    got = lax.ppermute(sent, "seq", swap)
    pair = kept + got
    far = lax.all_to_all(pair, "seq", 0, 0, axis_index_groups=groups)
    dq, dk, dv = backward(2, rate, offsets, e, dob, q, k, v, dqp, dkp, dvp, (pair,))
    grad_scale = 1.0 / math.sqrt(tok * seq_count * lax.axis_size("dp"))
    mine = total(far, 2 * rows, rows // chips, lax.axis_size("dp"), dk)
    mine = lax.all_to_all(mine, "dp", 0, 0)
    spread = lax.all_to_all(spread_sum(grad_scale, mine, seq_count), "seq", 0, 0)
    spread = spread.reshape((chips, 2) + spread.shape[1:])
    weight_grad = spread.transpose(0, 2, 1, 3).reshape(w_out.shape)
    dq, kg, vg, mixed = backward_last(
        rate, offsets, e, dob, q, k, v, dqp, dkp, dvp, far, dq, dk, dv, terms
    )
    return (mixed[None], dq[None], kg[None], vg[None], weight_grad)


def solution(mesh):
    full = P("dp", "head", "seq")
    return jax.shard_map(
        shards,
        mesh=mesh,
        in_specs=(full, full, full, full, P("head", None), P("dp"), P("head")),
        out_specs=(full, full, full, full, P("head", None)),
        check_vma=False,
    )
```
